256 devices in a mesh: tm: 64 (over y, z_lo, x, core), space: 4 (over z_hi).
Axes of the slice: x: 4, y: 4, z: 8 (z_hi: 4, z_lo: 2; z = z_hi * 2 + z_lo), core: 2. Of those that a mesh axis runs over, the one named last changes fastest.
Arguments:
- source: float32 [64, 128, 4096], P('tm', 'space'), may hold values from -6 to 6
- diffusivity: float32 [128, 4096], P('space'), may hold values from 0.2 to 2
Outputs:
- solution: float32 [64, 128, 4096], P('tm', 'space')
The draws below stay inside these ranges and needn't reach their ends.
All inputs are finite; a program needn't handle non-finite values.
Results may differ from the reference program's by a relative error of at most 0.0008.
Values sent between devices are 32-bit elements; how exact they have to be, the bound alone decides.
A program may use at most 64 MiB of HBM per device.

```python
import math
import jax
import jax.numpy as jnp
from jax import lax

NX = 4096
SWEEPS = 8
STEPS = 64
NY = 128


def level_of(own_key, extent, shards, low, largest):
    factor_of = 1.0
    for position, blocks in shards:
        heights = jax.random.uniform(jax.random.fold_in(jax.random.fold_in(own_key, 6), position), (blocks,), jnp.float32, low / len(shards), largest / len(shards))
        factor_of = factor_of * jnp.repeat(jnp.exp(heights), extent[position] // blocks).reshape((-1,) + (1,) * (len(extent) - 1 - position))
    return factor_of


def normal_values(key, shape, spread, limit, shards=(), held_as=jnp.bfloat16):
    factor_of = level_of(key, shape, shards, -0.22, 0.18) if shards else 1.0
    array = jax.random.normal(key, shape, jnp.float32) * spread * factor_of
    return jnp.minimum(jnp.maximum(array, -limit), limit).astype(held_as)


def setup_inputs(seed: int = 0) -> dict:
    streams_of = jax.random.split(jax.random.key(seed), 3)
    source = normal_values(streams_of[0], (STEPS, NY, NX), 1.0, 6.0, ((0, 64), (1, 4)), jnp.float32)
    diffusivity = jnp.clip(jnp.exp(math.log(2.0) - 2.3025851 * jax.random.uniform(streams_of[1], (NY, NX), jnp.float32) ** level_of(streams_of[1], (NY, NX), ((0, 4),), -0.2, 0.2)), 0.2, 2.0)
    return {"source": source, "diffusivity": diffusivity}


circulant_alpha = 0.01
step_ratio = 4.0
damping = 0.8


def face_terms(diffusivity):
    padded = jnp.pad(diffusivity, 1)
    c_north = 0.5 * (diffusivity + padded[:-2, 1:-1])
    c_south = 0.5 * (diffusivity + padded[2:, 1:-1])
    c_west = 0.5 * (diffusivity + padded[1:-1, :-2])
    c_east = 0.5 * (diffusivity + padded[1:-1, 2:])
    return c_north, c_south, c_west, c_east


def neighbour_sum(field, faces):
    c_north, c_south, c_west, c_east = faces
    padded = jnp.pad(field, ((0, 0), (1, 1), (1, 1)))
    return (c_north * padded[:, :-2, 1:-1] + c_south * padded[:, 2:, 1:-1]
            + c_west * padded[:, 1:-1, :-2] + c_east * padded[:, 1:-1, 2:])


def reference(source, diffusivity):
    length = STEPS
    faces = face_terms(diffusivity)
    coef_sum = faces[0] + faces[1] + faces[2] + faces[3]
    time_pos = jnp.arange(length, dtype=jnp.float32)
    alpha_root = circulant_alpha ** (1.0 / length)
    angle = 2.0 * math.pi * jnp.outer(time_pos, time_pos) / length
    weight = jnp.power(jnp.float32(circulant_alpha), time_pos / length)
    scaled = source * weight[:, None, None]
    spec_re = jnp.einsum("kn,nyx->kyx", jnp.cos(angle), scaled, precision=lax.Precision.HIGHEST)
    spec_im = -jnp.einsum("kn,nyx->kyx", jnp.sin(angle), scaled, precision=lax.Precision.HIGHEST)
    freq_angle = 2.0 * math.pi * time_pos / length
    lam_re = (1.0 - alpha_root * jnp.cos(freq_angle))[:, None, None]
    lam_im = (alpha_root * jnp.sin(freq_angle))[:, None, None]
    diag_re = lam_re + step_ratio * coef_sum[None]
    inv_norm = 1.0 / (diag_re * diag_re + lam_im * lam_im)

    def divide(res_re, res_im):
        return ((diag_re * res_re + lam_im * res_im) * inv_norm,
                (diag_re * res_im - lam_im * res_re) * inv_norm)

    iter_re, iter_im = divide(spec_re, spec_im)
    iter_re = damping * iter_re
    iter_im = damping * iter_im
    for sweep in range(SWEEPS - 1):
        near_re = neighbour_sum(iter_re, faces)
        near_im = neighbour_sum(iter_im, faces)
        apply_re = lam_re * iter_re - lam_im * iter_im + step_ratio * (coef_sum * iter_re - near_re)
        apply_im = lam_re * iter_im + lam_im * iter_re + step_ratio * (coef_sum * iter_im - near_im)
        upd_re, upd_im = divide(spec_re - apply_re, spec_im - apply_im)
        iter_re = iter_re + damping * upd_re
        iter_im = iter_im + damping * upd_im
    back = jnp.power(jnp.float32(circulant_alpha), -time_pos / length) / length
    timed = (jnp.einsum("nk,kyx->nyx", jnp.cos(angle), iter_re, precision=lax.Precision.HIGHEST)
             - jnp.einsum("nk,kyx->nyx", jnp.sin(angle), iter_im, precision=lax.Precision.HIGHEST))
    return timed * back[:, None, None]
```

```python
import math

import jax
import jax.numpy as jnp
import numpy as np
from jax import lax
from jax.experimental import pallas as pl
from jax.experimental.pallas import tpu as pltpu
from jax.sharding import PartitionSpec as P

SWEEPS = 8
STEPS = 64
circulant_alpha = 0.01
step_ratio = 4.0
damping = 0.8

MESH = pl.DeviceIdType.MESH
F32 = jnp.float32
BF16 = jnp.bfloat16
ROWS = 16
COLS = 128
HALF = STEPS // 2
FOLD = 16
WIDE = 80
PAD = 8
INNER = pl.ds(PAD, WIDE)


def tables():
    steps = np.arange(STEPS)
    freq = np.arange(HALF)
    angle = 2.0 * math.pi * np.outer(steps, freq) / STEPS
    weight = circulant_alpha ** (steps / STEPS)
    real, imag = np.cos(angle), -np.sin(angle)
    imag[:, 0] = np.cos(math.pi * steps)
    twice = np.where(freq == 0, 1.0, 2.0)
    ahead = weight[:, None] / step_ratio
    back = (1.0 / weight / STEPS)[:, None] * twice
    forward = np.zeros((4 * STEPS, 8 * HALF))
    inverse = np.zeros((2 * STEPS, 8 * HALF))
    for side in range(2):
        for part in range(2):
            group = 2 * side + part
            rows = slice((2 * part + side) * STEPS, (2 * part + side + 1) * STEPS)
            re = slice(group * HALF, (group + 1) * HALF)
            im = slice((4 + group) * HALF, (5 + group) * HALF)
            forward[rows, re] = real * ahead
            forward[rows, im] = imag * ahead
            rows = slice(side * STEPS, (side + 1) * STEPS)
            inverse[rows, re] = real * back
            inverse[rows, im] = imag * back
    root = circulant_alpha ** (1.0 / STEPS)
    theta = 2.0 * math.pi * freq / STEPS
    lam_re = 1.0 - root * np.cos(theta)
    lam_im = root * np.sin(theta)
    lam_im[0] = 0.0
    other = lam_re.copy()
    other[0] = 1.0 + root
    lam = np.zeros((8, 4 * HALF), np.float32)
    lam[0] = np.tile(lam_re, 4)
    lam[1] = np.tile(other, 4)
    lam[2] = np.tile(lam_im, 4)

    def split(array, axis):
        array = np.asarray(array, np.float32)
        high = array.astype(jnp.bfloat16)
        low = (array - high.astype(np.float32)).astype(jnp.bfloat16)
        return np.concatenate([high, high, low], axis=axis)

    return split(forward, 0), split(inverse, 1), lam


def place(t):
    return t // 16, (t // 8) % 2, (t // 2) % 4, t % 2


def column_of(t):
    y, _, x, core = place(t)
    along = x + (y % 2) * (3 - 2 * x)
    return (y * 4 + along) * 2 + core


def device_of(column, zl):
    y = column // 8
    along = (column // 2) % 4
    x = along + (y % 2) * (3 - 2 * along)
    return y * 16 + zl * 8 + x * 2 + column % 2


def part_of(value):
    return (lax.broadcasted_iota(jnp.int32, value.shape, value.ndim - 1) // 32) % 2


def swap_parts(value):
    axis = value.ndim - 1
    return jnp.where(part_of(value) == 0, pltpu.roll(value, 96, axis), pltpu.roll(value, 32, axis))


def halves(value):
    high = value.astype(BF16)
    low = (value - high.astype(F32)).astype(BF16)
    return high, low


def body(src, dif, fwd_hbm, inv_hbm, lam_hbm, out, *refs):
    (fwd, inv, lam, recv, top, bottom, kap, knear, kwide, kfold, plink, qplus, qminus,
     gr, gs, gi, lhs, sr, si, pack_l, pack_r, got_l, got_r, send) = refs[:24]
    fr, fi = refs[24 : 24 + SWEEPS], refs[24 + SWEEPS : 24 + 2 * SWEEPS]
    (in_send, in_recv, z_send, z_recv, k_send, k_recv, c_send, c_recv, out_send, out_recv,
     load_sem, near_sem) = refs[24 + 2 * SWEEPS :]
    t = lax.axis_index("tm")
    s = lax.axis_index("space")
    y, zl, x, _ = place(t)
    col = column_of(t)
    z = s * 2 + zl

    def z_device(step):
        other = (z + step + 8) % 8
        return (t + (other % 2 - zl) * 8, other // 2)

    outer = z_device(2 * zl - 1)

    def tile(index):
        return pl.ds(pl.multiple_of(index * COLS, COLS), COLS)

    def rows16(index):
        return pl.ds(pl.multiple_of(index * ROWS, ROWS), ROWS)

    barrier = pltpu.get_barrier_semaphore()

    @pl.loop(1, STEPS)
    def _(d):
        pl.semaphore_signal(barrier, inc=1, device_id=((t + d) % STEPS, s), device_id_type=MESH)

    pl.semaphore_signal(barrier, inc=1, device_id=outer, device_id_type=MESH)
    loads = [
        pltpu.make_async_copy(a, b, load_sem.at[i])
        for i, (a, b) in enumerate(((fwd_hbm, fwd), (inv_hbm, inv), (lam_hbm, lam)))
    ]
    loads += [
        pltpu.make_async_copy(
            dif.at[pl.ds(pl.multiple_of(zl * 8, 8), 24), tile((col + 31 + d) % 32)],
            knear.at[:, pl.ds(d * COLS, COLS)],
            near_sem.at[d],
        )
        for d in range(3)
    ]
    for c in loads:
        c.start()
    pl.semaphore_wait(barrier, STEPS)

    def arriving(p):
        _, pzl, _, _ = place(p)
        return pltpu.make_async_remote_copy(
            src_ref=src.at[rows16(pzl), tile(column_of(p))],
            dst_ref=recv.at[t],
            send_sem=in_send, recv_sem=in_recv.at[y],
            device_id=(p, s), device_id_type=MESH,
        )

    def partner(d):
        phase, py, low = d // 16, (d // 4) % 4, d % 4
        px = (phase - y + py + 4) % 4
        return py * 16 + (low // 2) * 8 + px * 2 + low % 2

    krow = pl.ds(pl.multiple_of(zl * 24, 8), 8)
    kcopies = [
        pltpu.make_async_remote_copy(
            src_ref=dif.at[krow, tile((col + 31 + d) % 32)],
            dst_ref=kap.at[:, pl.ds(d * COLS, COLS)],
            send_sem=k_send.at[d], recv_sem=k_recv.at[d],
            device_id=outer, device_id_type=MESH,
        )
        for d in range(3)
    ]
    for c in kcopies:
        c.start()

    @pl.loop(0, STEPS)
    def _(d):
        p = partner(d)

        @pl.when(p != t)
        def _():
            arriving(p).start()

    own = pltpu.make_async_copy(src.at[rows16(zl), tile(col)], recv.at[t], in_recv.at[y])
    own.start()

    for c in loads:
        c.wait()
    for c in kcopies:
        c.wait()
    row_id = lax.broadcasted_iota(jnp.int32, (32, COLS), 0)
    low_ok = jnp.where(z > 0, 0, 8)
    high_ok = jnp.where(z < 7, 32, 24)
    for d in range(3):
        near24 = knear[:, d * COLS : (d + 1) * COLS]
        far8 = kap[:, d * COLS : (d + 1) * COLS]
        strip = jnp.where(
            zl == 0, jnp.concatenate([far8, near24], 0), jnp.concatenate([near24, far8], 0)
        )
        keep = (row_id >= low_ok) & (row_id < high_ok)
        if d == 0:
            keep = keep & (col > 0)
        if d == 2:
            keep = keep & (col < 31)
        strip = jnp.where(keep, strip, 0.0)
        strip = jnp.concatenate([strip, jnp.zeros((96, COLS), F32)], 0)
        kwide[pl.ds(d * COLS, COLS), :] = strip.T
    kfold[...] = jnp.zeros(kfold.shape, F32)
    edge = jnp.zeros((FOLD + 1, PAD, 128), F32)
    for ref in fr[:-1] + fi[:-1]:
        ref[:, pl.ds(0, PAD), :] = edge
        ref[:, pl.ds(PAD + WIDE, PAD), :] = edge
    lane = lax.broadcasted_iota(jnp.int32, (WIDE, 128), 1)
    is_a = lane < 64
    is_0 = lane % 64 < 32
    part0 = kwide[pl.ds(COLS - 8, WIDE), :]
    part1 = kwide[pl.ds(COLS + 56, WIDE), :]
    for j in range(FOLD):
        k = 31 - j
        kfold[j, INNER, :] = jnp.where(
            is_a,
            jnp.where(is_0, part0[:, j : j + 1], part1[:, j : j + 1]),
            jnp.where(is_0, part0[:, k : k + 1], part1[:, k : k + 1]),
        )
    kfold[FOLD, INNER, :] = pltpu.roll(kfold[FOLD - 1, INNER, :], 64, 1)
    lam_re = lam[0:1, :]
    lam_other = lam[1:2, :]
    lam_im = lam[2:3, :]
    plink[0] = kfold[0, INNER, :]

    @pl.loop(0, FOLD)
    def _(j):
        here = kfold[j, INNER, :]
        south = 0.5 * (here + kfold[j + 1, INNER, :])
        east = 0.5 * (here + kfold[j, pl.ds(PAD + 1, WIDE), :])
        west = 0.5 * (here + kfold[j, pl.ds(PAD - 1, WIDE), :])
        plink[j + 1] = south
        qplus[j] = east
        qminus[j] = west
        total = step_ratio * (plink[j] + south + east + west)
        inside = jnp.where(here > 0.0, damping * step_ratio, 0.0)
        diag = lam_re + total
        scale = inside / (diag * diag + lam_im * lam_im)
        gr[j] = scale * diag
        gi[j] = scale * lam_im
        diag = lam_other + total
        gs[j] = inside * diag / (diag * diag + lam_im * lam_im)

    def blocks(count, send_sem, recv_sem):
        some = recv.at[pl.ds(0, count)]
        return pltpu.make_async_remote_copy(
            src_ref=some, dst_ref=some, send_sem=send_sem, recv_sem=recv_sem,
            device_id=outer, device_id_type=MESH,
        )

    zcopies = []
    for phase in range(4):
        group = (phase + y - x + 4) % 4
        blocks(16, in_send, in_recv.at[group]).wait_recv()
        steps = pl.ds(group * 16, 16)
        pair = [
            pltpu.make_async_remote_copy(
                src_ref=recv.at[steps, pl.ds(0, 8), :], dst_ref=bottom.at[steps],
                send_sem=z_send.at[phase, 0], recv_sem=z_recv.at[phase, 0],
                device_id=z_device(-1), device_id_type=MESH,
            ),
            pltpu.make_async_remote_copy(
                src_ref=recv.at[steps, pl.ds(8, 8), :], dst_ref=top.at[steps],
                send_sem=z_send.at[phase, 1], recv_sem=z_recv.at[phase, 1],
                device_id=z_device(1), device_id_type=MESH,
            ),
        ]
        zcopies += pair
        for c in pair:
            c.start()

    left = device_of((col + 31) % 32, zl)
    right = device_of((col + 1) % 32, zl)

    def fold_in(i, first, second):
        high, low = halves(jnp.concatenate([first, second], 0).T)
        pieces = [high[:64], high[64:], low[:64], low[64:], high[:64], high[64:]]
        lhs[pl.ds(pl.multiple_of(i * 64, 64), 64), :] = jnp.concatenate(pieces, 1)

    def transformed(start, stage):
        result = jnp.dot(lhs[...], fwd[...], preferred_element_type=F32)
        sr[pl.ds(start, 8), pl.ds(8, 64), :] = result[:, :128].reshape(8, 64, 128)
        si[pl.ds(start, 8), pl.ds(8, 64), :] = result[:, 128:].reshape(8, 64, 128)
        mine = pl.ds(start, 8)
        re, im = sr[mine, pl.ds(8, 8), :], si[mine, pl.ds(8, 8), :]
        pack_l[mine] = jnp.where(part_of(re) == 0, re, swap_parts(im))
        re, im = sr[mine, pl.ds(64, 8), :], si[mine, pl.ds(64, 8), :]
        pack_r[mine] = jnp.where(part_of(re) == 1, re, swap_parts(im))
        copies = [
            pltpu.make_async_remote_copy(
                src_ref=pack_l.at[mine], dst_ref=got_r.at[mine],
                send_sem=c_send.at[stage, 0], recv_sem=c_recv.at[stage, 0],
                device_id=(left, s), device_id_type=MESH,
            ),
            pltpu.make_async_remote_copy(
                src_ref=pack_r.at[mine], dst_ref=got_l.at[mine],
                send_sem=c_send.at[stage, 1], recv_sem=c_recv.at[stage, 1],
                device_id=(right, s), device_id_type=MESH,
            ),
        ]
        for c in copies:
            c.start()
        return copies

    def first_level(start, copies):
        for c in copies:
            c.wait()

        @pl.loop(start, start + 8)
        def _(j):
            re, im, x = sr[j, pl.ds(64, 8), :], si[j, pl.ds(64, 8), :], got_l[j]
            sr[j, pl.ds(0, 8), :] = swap_parts(jnp.where(part_of(x) == 1, x, re))
            si[j, pl.ds(0, 8), :] = jnp.where(part_of(x) == 0, x, swap_parts(im))
            re, im, x = sr[j, pl.ds(8, 8), :], si[j, pl.ds(8, 8), :], got_r[j]
            sr[j, pl.ds(72, 8), :] = swap_parts(jnp.where(part_of(x) == 0, x, re))
            si[j, pl.ds(72, 8), :] = jnp.where(part_of(x) == 1, x, swap_parts(im))
            re, im, cross = sr[j], si[j], gi[j]
            fr[0][j, INNER, :] = gr[j] * re + cross * im
            fi[0][j, INNER, :] = gs[j] * im - cross * re

    def seam(level):
        for ref in (fr[level], fi[level]):
            ref[FOLD, INNER, :] = pltpu.roll(ref[FOLD - 1, INNER, :], 64, 1)

    def sweep(level, first, last):
        pr, pi, nr, ni = fr[level - 1], fi[level - 1], fr[level], fi[level]

        @pl.loop(first, last)
        def _(j):
            for q in range(2):
                at, mid = pl.ds(40 * q, 40), pl.ds(PAD + 40 * q, 40)
                west, east = pl.ds(PAD - 1 + 40 * q, 40), pl.ds(PAD + 1 + 40 * q, 40)
                p0, p1, q0, q1 = plink[j, at, :], plink[j + 1, at, :], qminus[j, at, :], qplus[j, at, :]
                vr = sr[j, at, :] + p0 * pr[j - 1, mid, :] + p1 * pr[j + 1, mid, :]
                vr = vr + (q0 * pr[j, west, :] + q1 * pr[j, east, :])
                vi = si[j, at, :] + p0 * pi[j - 1, mid, :] + p1 * pi[j + 1, mid, :]
                vi = vi + (q0 * pi[j, west, :] + q1 * pi[j, east, :])
                cross = gi[j, at, :]
                nr[j, mid, :] = (1.0 - damping) * pr[j, mid, :] + (gr[j, at, :] * vr + cross * vi)
                ni[j, mid, :] = (1.0 - damping) * pi[j, mid, :] + (gs[j, at, :] * vi - cross * vr)

    recv2 = recv.reshape(STEPS * ROWS, COLS)

    @pl.loop(0, 8)
    def _(i):
        fold_in(i, recv2[pl.ds(i, STEPS, stride=ROWS), :], recv2[pl.ds(15 - i, STEPS, stride=ROWS), :])

    inside = transformed(8, 0)
    for c in zcopies:
        c.wait()
    top2 = top.reshape(STEPS * 8, COLS)
    bottom2 = bottom.reshape(STEPS * 8, COLS)

    @pl.loop(0, 8)
    def _(h):
        fold_in(h, top2[pl.ds(h, STEPS, stride=8), :], bottom2[pl.ds(7 - h, STEPS, stride=8), :])

    outside = transformed(0, 1)
    first_level(8, inside)
    seam(0)
    for level in range(1, SWEEPS):
        sweep(level, 8 + level, FOLD)
        if level < SWEEPS - 1:
            seam(level)
    first_level(0, outside)
    for level in range(1, SWEEPS):
        sweep(level, level + 1, 8 + level)

    send2 = send.reshape(STEPS * ROWS, COLS)
    middle = pl.ds(PAD + 8, 64)
    in_part0 = part_of(jnp.zeros((64, 256), BF16)) == 0

    @pl.loop(0, 8)
    def _(i):
        both = jnp.concatenate([fr[-1][8 + i, middle, :], fi[-1][8 + i, middle, :]], 1)
        low_cols = jnp.where(in_part0, both, 0.0)
        both = jnp.concatenate([low_cols, both - low_cols], 0)
        high, low = halves(both)
        result = lax.dot_general(
            inv[...], jnp.concatenate([high, low, high], 1), (((1,), (1,)), ((), ())),
            preferred_element_type=F32,
        )
        send2[pl.ds(i, STEPS, stride=ROWS), :] = result[:STEPS]
        send2[pl.ds(15 - i, STEPS, stride=ROWS), :] = result[STEPS:]

    def leaving(p):
        return pltpu.make_async_remote_copy(
            src_ref=send.at[p],
            dst_ref=out.at[rows16(zl), tile(col)],
            send_sem=out_send, recv_sem=out_recv,
            device_id=(p, s), device_id_type=MESH,
        )

    @pl.loop(0, STEPS)
    def _(d):
        p = partner(d)

        @pl.when(p != t)
        def _():
            leaving(p).start()

    out[rows16(zl), tile(col)] = send[t]
    blocks(STEPS - 1, in_send, out_recv).wait_send()
    blocks(STEPS - 1, out_send, out_recv).wait_send()
    blocks(STEPS - 1, out_send, out_recv).wait_recv()


def per_device(source, diffusivity):
    fwd, inv, lam = (jnp.asarray(a) for a in tables())
    dma = pltpu.SemaphoreType.DMA

    def vmem(*shape):
        return pltpu.VMEM(shape, F32)

    level = vmem(FOLD + 1, WIDE + 2 * PAD, 128)
    plane = vmem(FOLD, WIDE, 128)
    edge = vmem(FOLD, 8, 128)
    result = pl.pallas_call(
        body,
        out_shape=jax.ShapeDtypeStruct(source.shape[1:], F32),
        in_specs=[pl.BlockSpec(memory_space=pl.ANY)] * 5,
        out_specs=pl.BlockSpec(memory_space=pltpu.VMEM),
        scratch_shapes=[
            pltpu.VMEM(fwd.shape, BF16), pltpu.VMEM(inv.shape, BF16), vmem(*lam.shape),
            vmem(STEPS, ROWS, COLS), vmem(STEPS, 8, COLS), vmem(STEPS, 8, COLS),
            vmem(8, 3 * COLS), vmem(24, 3 * COLS), vmem(3 * COLS, 128),
            level, vmem(FOLD + 1, WIDE, 128), plane, plane, plane, plane, plane,
            pltpu.VMEM((512, 768), BF16), plane, plane, edge, edge, edge, edge,
            vmem(STEPS, ROWS, COLS),
        ]
        + [level] * (2 * SWEEPS)
        + [
            dma, dma((4,)), dma((4, 2)), dma((4, 2)), dma((3,)), dma((3,)), dma((2, 2)), dma((2, 2)),
            dma, dma, dma((3,)), dma((3,)),
        ],
        compiler_params=pltpu.CompilerParams(
            collective_id=0, has_side_effects=True, vmem_limit_bytes=56 * 2**20
        ),
        cost_estimate=pl.CostEstimate(flops=10**8, bytes_accessed=2**21, transcendentals=0),
    )(source[0], diffusivity, fwd, inv, lam)
    return result[None]


def solution(mesh):
    return jax.shard_map(
        per_device,
        mesh=mesh,
        in_specs=(P("tm", "space", None), P("space", None)),
        out_specs=P("tm", "space", None),
        check_vma=False,
    )
```

```python
import math

import jax
import jax.numpy as jnp
from jax import lax
from jax.experimental import pallas as pl
from jax.experimental.pallas import tpu as pltpu
from jax.sharding import PartitionSpec as P

SWEEPS = 8
STEPS = 64
circulant_alpha = 0.01
step_ratio = 4.0
damping = 0.8

MESH = pl.DeviceIdType.MESH
F32 = jnp.float32
BF16 = jnp.bfloat16
ROWS = 16
COLS = 128
HALF = STEPS // 2
FOLD = 16
WIDE = 80
PAD = 8
INNER = pl.ds(PAD, WIDE)


def iota(shape, axis):
    return lax.broadcasted_iota(jnp.int32, shape, axis)


def wave(steps, freq, imaginary):
    turn = jnp.where(imaginary, jnp.where(freq == 0, HALF * steps, steps * freq + STEPS // 4), steps * freq)
    return jnp.cos((turn % STEPS).astype(F32) * (2.0 * math.pi / STEPS))


def power(steps, sign):
    return jnp.exp(steps.astype(F32) * (sign * math.log(circulant_alpha) / STEPS))


def fill_forward(ref):
    shape = (STEPS, 8 * HALF)
    lane = iota(shape, 1)
    steps = iota(shape, 0)
    table = wave(steps, lane % HALF, lane >= 4 * HALF) * power(steps, 1.0) * (1.0 / step_ratio)
    for block in range(4):
        mine = (lane // HALF) % 4 == (block % 2) * 2 + block // 2
        high, low = halves(jnp.where(mine, table, 0.0))
        for base, value in ((0, high), (256, high), (512, low)):
            ref[pl.ds(base + block * STEPS, STEPS), :] = value


def fill_inverse(ref):
    shape = (4 * HALF, 4 * STEPS)
    row = iota(shape, 0)
    lane = iota(shape, 1)
    freq, steps, block = row % HALF, lane % STEPS, lane // STEPS
    mine = row // HALF == (block % 2) * 2 + block // 2
    scale = power(steps, -1.0) * jnp.where(mine, jnp.where(freq == 0, 1.0, 2.0) / STEPS, 0.0)
    for plane in range(2):
        high, low = halves(wave(steps, freq, plane == 1) * scale)
        for base, value in ((0, high), (256, high), (512, low)):
            ref[pl.ds(base + plane * 128, 128), :] = value


def place(t):
    return t // 16, (t // 8) % 2, (t // 2) % 4, t % 2


def column_of(t):
    y, _, x, core = place(t)
    along = x + (y % 2) * (3 - 2 * x)
    return (y * 4 + along) * 2 + core


def device_of(column, zl):
    y = column // 8
    along = (column // 2) % 4
    x = along + (y % 2) * (3 - 2 * along)
    return y * 16 + zl * 8 + x * 2 + column % 2


def part_of(value):
    return (lax.broadcasted_iota(jnp.int32, value.shape, value.ndim - 1) // 32) % 2


def swap_parts(value):
    axis = value.ndim - 1
    return jnp.where(part_of(value) == 0, pltpu.roll(value, 96, axis), pltpu.roll(value, 32, axis))


def halves(value):
    high = value.astype(BF16)
    low = (value - high.astype(F32)).astype(BF16)
    return high, low


def body(src, dif, out, *refs):
    (fwd, inv, back, recv, top, bottom, kap, knear, kwide, kfold, plink, qplus, qminus,
     gr, gs, gi, lhs, sr, si, pack_l, pack_r, got_l, got_r, send) = refs[:24]
    fr, fi = refs[24 : 24 + SWEEPS], refs[24 + SWEEPS : 24 + 2 * SWEEPS]
    (in_send, in_recv, z_send, z_recv, k_send, k_recv, c_send, c_recv, out_send, out_recv,
     near_sem, mine_sem) = refs[24 + 2 * SWEEPS :]
    t = lax.axis_index("tm")
    s = lax.axis_index("space")
    y, zl, x, _ = place(t)
    col = column_of(t)
    z = s * 2 + zl

    def z_device(step):
        other = (z + step + 8) % 8
        return (t + (other % 2 - zl) * 8, other // 2)

    outer = z_device(2 * zl - 1)

    def tile(index):
        return pl.ds(pl.multiple_of(index * COLS, COLS), COLS)

    def rows16(index):
        return pl.ds(pl.multiple_of(index * ROWS, ROWS), ROWS)

    barrier = pltpu.get_barrier_semaphore()

    @pl.loop(1, STEPS)
    def _(d):
        pl.semaphore_signal(barrier, inc=1, device_id=((t + d) % STEPS, s), device_id_type=MESH)

    above, below = z > 0, z < 7
    has_outer = above & below

    @pl.when(has_outer)
    def _():
        pl.semaphore_signal(barrier, inc=1, device_id=outer, device_id_type=MESH)

    loads = [
        pltpu.make_async_copy(
            dif.at[pl.ds(pl.multiple_of(zl * 8, 8), 24), tile((col + 31 + d) % 32)],
            knear.at[:, pl.ds(d * COLS, COLS)],
            near_sem.at[d],
        )
        for d in range(3)
    ]
    for c in loads:
        c.start()
    pl.semaphore_wait(barrier, STEPS - 1 + has_outer.astype(jnp.int32))

    def arriving(p):
        _, pzl, _, _ = place(p)
        return pltpu.make_async_remote_copy(
            src_ref=src.at[rows16(pzl), tile(column_of(p))],
            dst_ref=recv.at[t],
            send_sem=in_send, recv_sem=in_recv.at[y],
            device_id=(p, s), device_id_type=MESH,
        )

    krow = pl.ds(pl.multiple_of(zl * 24, 8), 8)
    kcopies = [
        pltpu.make_async_remote_copy(
            src_ref=dif.at[krow, tile((col + 31 + d) % 32)],
            dst_ref=kap.at[:, pl.ds(d * COLS, COLS)],
            send_sem=k_send.at[d], recv_sem=k_recv.at[d],
            device_id=outer, device_id_type=MESH,
        )
        for d in range(3)
    ]
    @pl.when(has_outer)
    def _():
        for c in kcopies:
            c.start()


    @pl.loop(1, STEPS)
    def _(d):
        arriving((t + d) % STEPS).start()

    own = pltpu.make_async_copy(src.at[rows16(zl), tile(col)], recv.at[t], in_recv.at[y])
    own.start()

    def blocks(count, send_sem, recv_sem):
        some = recv.at[pl.ds(0, count)]
        return pltpu.make_async_remote_copy(
            src_ref=some, dst_ref=some, send_sem=send_sem, recv_sem=recv_sem,
            device_id=outer, device_id_type=MESH,
        )

    def link(j):
        here = kfold[j, INNER, :]
        south = 0.5 * (here + kfold[j + 1, INNER, :])
        east = 0.5 * (here + kfold[j, pl.ds(PAD + 1, WIDE), :])
        west = 0.5 * (here + kfold[j, pl.ds(PAD - 1, WIDE), :])
        plink[j + 1] = south
        qplus[j] = east
        qminus[j] = west
        total = step_ratio * (plink[j] + south + east + west)
        inside = jnp.where(here > 0.0, damping * step_ratio, 0.0)
        diag = lam_re + total
        scale = inside / (diag * diag + lam_im * lam_im)
        gr[j] = scale * diag
        gi[j] = scale * lam_im
        diag = lam_other + total
        gs[j] = inside * diag / (diag * diag + lam_im * lam_im)

    def gather_coefficients():
        for c in loads:
            c.wait()
        @pl.when(has_outer)
        def _():
            for c in kcopies:
                c.wait()

        row_id = lax.broadcasted_iota(jnp.int32, (32, COLS), 0)
        low_ok = jnp.where(z > 0, 0, 8)
        high_ok = jnp.where(z < 7, 32, 24)
        for d in range(3):
            near24 = knear[:, d * COLS : (d + 1) * COLS]
            far8 = kap[:, d * COLS : (d + 1) * COLS]
            strip = jnp.where(
                zl == 0, jnp.concatenate([far8, near24], 0), jnp.concatenate([near24, far8], 0)
            )
            keep = (row_id >= low_ok) & (row_id < high_ok)
            if d == 0:
                keep = keep & (col > 0)
            if d == 2:
                keep = keep & (col < 31)
            strip = jnp.where(keep, strip, 0.0)
            strip = jnp.concatenate([strip, jnp.zeros((96, COLS), F32)], 0)
            kwide[pl.ds(d * COLS, COLS), :] = strip.T
        for at in (pl.ds(0, PAD), pl.ds(PAD + WIDE, PAD)):
            kfold[:, at, :] = jnp.zeros((FOLD + 1, PAD, 128), F32)
        lane = lax.broadcasted_iota(jnp.int32, (WIDE, 128), 1)
        is_a = lane < 64
        is_0 = lane % 64 < 32
        part0 = kwide[pl.ds(COLS - 8, WIDE), :]
        part1 = kwide[pl.ds(COLS + 56, WIDE), :]
        for j in range(FOLD):
            k = 31 - j
            kfold[j, INNER, :] = jnp.where(
                is_a,
                jnp.where(is_0, part0[:, j : j + 1], part1[:, j : j + 1]),
                jnp.where(is_0, part0[:, k : k + 1], part1[:, k : k + 1]),
            )
        kfold[FOLD, INNER, :] = pltpu.roll(kfold[FOLD - 1, INNER, :], 64, 1)

    def clear_edges():
        for missing, ref in ((z == 0, top), (z == 7, bottom)):

            @pl.when(missing)
            def _():
                ref[...] = jnp.zeros(ref.shape, F32)

        edge = jnp.zeros((FOLD + 1, PAD, 128), F32)
        for ref in fr[:-1] + fi[:-1]:
            ref[:, pl.ds(0, PAD), :] = edge
            ref[:, pl.ds(PAD + WIDE, PAD), :] = edge

    slot = iota((1, 128), 1) % HALF
    root = circulant_alpha ** (1.0 / STEPS)
    theta = slot.astype(F32) * (2.0 * math.pi / STEPS)
    lam_re = 1.0 - root * jnp.cos(theta)
    lam_im = root * jnp.sin(theta)
    lam_other = jnp.where(slot == 0, 1.0 + root, lam_re)


    def links(first, last):
        @pl.loop(first, last)
        def _(j):
            link(j)

    def prepare(phase):
        if phase == 0:
            gather_coefficients()
            plink[0] = kfold[0, INNER, :]
        elif phase == 1:
            links(0, 8)
        elif phase == 2:
            links(8, FOLD)
        else:
            clear_edges()
            fill_forward(fwd)

    zcopies = []
    for phase in range(4):
        prepare(phase)
        group = (y + 3 - phase) % 4
        blocks(16, in_send, in_recv.at[group]).wait_recv()
        steps = pl.ds(group * 16, 16)
        pair = [
            pltpu.make_async_remote_copy(
                src_ref=recv.at[steps, pl.ds(0, 8), :], dst_ref=bottom.at[steps],
                send_sem=z_send.at[phase, 0], recv_sem=z_recv.at[phase, 0],
                device_id=z_device(-1), device_id_type=MESH,
            ),
            pltpu.make_async_remote_copy(
                src_ref=recv.at[steps, pl.ds(8, 8), :], dst_ref=top.at[steps],
                send_sem=z_send.at[phase, 1], recv_sem=z_recv.at[phase, 1],
                device_id=z_device(1), device_id_type=MESH,
            ),
        ]
        zcopies.append(pair)
        pl.when(above)(pair[0].start)
        pl.when(below)(pair[1].start)

    left = device_of((col + 31) % 32, zl)
    right = device_of((col + 1) % 32, zl)

    def fold_in(i, first, second):
        high, low = halves(jnp.concatenate([first, second], 0).T)
        pieces = [high[:64], high[64:], low[:64], low[64:], high[:64], high[64:]]
        lhs[pl.ds(i * 64, 64), :] = jnp.concatenate(pieces, 1)

    def transformed(start, stage):
        result = jnp.dot(lhs[...], fwd[...], preferred_element_type=F32)
        sr[pl.ds(start, 8), pl.ds(8, 64), :] = result[:, :128].reshape(8, 64, 128)
        si[pl.ds(start, 8), pl.ds(8, 64), :] = result[:, 128:].reshape(8, 64, 128)
        mine = pl.ds(start, 8)
        re, im = sr[mine, pl.ds(8, 8), :], si[mine, pl.ds(8, 8), :]
        pack_l[mine] = jnp.where(part_of(re) == 0, re, swap_parts(im))
        re, im = sr[mine, pl.ds(64, 8), :], si[mine, pl.ds(64, 8), :]
        pack_r[mine] = jnp.where(part_of(re) == 1, re, swap_parts(im))
        copies = [
            pltpu.make_async_remote_copy(
                src_ref=pack_l.at[mine], dst_ref=got_r.at[mine],
                send_sem=c_send.at[stage, 0], recv_sem=c_recv.at[stage, 0],
                device_id=(left, s), device_id_type=MESH,
            ),
            pltpu.make_async_remote_copy(
                src_ref=pack_r.at[mine], dst_ref=got_l.at[mine],
                send_sem=c_send.at[stage, 1], recv_sem=c_recv.at[stage, 1],
                device_id=(right, s), device_id_type=MESH,
            ),
        ]
        for c in copies:
            c.start()
        return copies

    def join(j, from_left, from_right):
        re, im = sr[j, pl.ds(64, 8), :], si[j, pl.ds(64, 8), :]
        part = part_of(re)
        sr[j, pl.ds(0, 8), :] = swap_parts(jnp.where(part == 1, from_left, re))
        si[j, pl.ds(0, 8), :] = jnp.where(part == 0, from_left, swap_parts(im))
        re, im = sr[j, pl.ds(8, 8), :], si[j, pl.ds(8, 8), :]
        sr[j, pl.ds(72, 8), :] = swap_parts(jnp.where(part == 0, from_right, re))
        si[j, pl.ds(72, 8), :] = jnp.where(part == 1, from_right, swap_parts(im))

    def first_level(j, start, size):
        at = pl.ds(start, size)
        re, im, cross = sr[j, at, :], si[j, at, :], gi[j, at, :]
        fr[0][j, pl.ds(PAD + start, size), :] = gr[j, at, :] * re + cross * im
        fi[0][j, pl.ds(PAD + start, size), :] = gs[j, at, :] * im - cross * re

    def seam(level):
        for ref in (fr[level], fi[level]):
            ref[FOLD, INNER, :] = pltpu.roll(ref[FOLD - 1, INNER, :], 64, 1)

    def sweep(level, first, last, edges=False):
        pr, pi, nr, ni = fr[level - 1], fi[level - 1], fr[level], fi[level]
        if level == SWEEPS - 1:
            spans = ((8, 8), (64, 8)) if edges else ((8, 32), (40, 32))
        else:
            spans = ((0, 16), (64, 16)) if edges else ((0, 40), (40, 40))

        @pl.loop(first, last)
        def _(j):
            for start, size in spans:
                at, mid = pl.ds(start, size), pl.ds(PAD + start, size)
                west, east = pl.ds(PAD - 1 + start, size), pl.ds(PAD + 1 + start, size)
                p0, p1, q0, q1 = plink[j, at, :], plink[j + 1, at, :], qminus[j, at, :], qplus[j, at, :]
                vr = sr[j, at, :] + p0 * pr[j - 1, mid, :] + p1 * pr[j + 1, mid, :]
                vr = vr + (q0 * pr[j, west, :] + q1 * pr[j, east, :])
                vi = si[j, at, :] + p0 * pi[j - 1, mid, :] + p1 * pi[j + 1, mid, :]
                vi = vi + (q0 * pi[j, west, :] + q1 * pi[j, east, :])
                cross = gi[j, at, :]
                nr[j, mid, :] = (1.0 - damping) * pr[j, mid, :] + (gr[j, at, :] * vr + cross * vi)
                ni[j, mid, :] = (1.0 - damping) * pi[j, mid, :] + (gs[j, at, :] * vi - cross * vr)

    recv2 = recv.reshape(STEPS * ROWS, COLS)

    for i in range(8):
        fold_in(i, recv2[pl.ds(i, STEPS, stride=ROWS), :], recv2[pl.ds(15 - i, STEPS, stride=ROWS), :])

    inside = transformed(8, 0)
    fill_inverse(inv)
    for c in inside:
        c.wait()

    @pl.loop(8, FOLD)
    def _(j):
        join(j, got_l[j], got_r[j])
        first_level(j, 0, WIDE)

    seam(0)
    for level in range(1, SWEEPS):
        sweep(level, 8 + level, FOLD)
        if level < SWEEPS - 1:
            seam(level)

    for up, down in zcopies:

        @pl.when(above)
        def _():
            up.wait_send()
            down.wait_recv()

        @pl.when(below)
        def _():
            down.wait_send()
            up.wait_recv()

    top2 = top.reshape(STEPS * 8, COLS)
    bottom2 = bottom.reshape(STEPS * 8, COLS)

    for h in range(8):
        fold_in(h, top2[pl.ds(h, STEPS, stride=8), :], bottom2[pl.ds(7 - h, STEPS, stride=8), :])

    outside = transformed(0, 1)

    @pl.loop(0, 8)
    def _(j):
        nothing = jnp.zeros((8, 128), F32)
        join(j, nothing, nothing)
        first_level(j, 0, WIDE)

    for level in range(1, SWEEPS):
        sweep(level, level + 1, 8 + level)
    for c in outside:
        c.wait()

    @pl.loop(0, 8)
    def _(j):
        join(j, got_l[j], got_r[j])
        first_level(j, 0, 16)
        first_level(j, 64, 16)

    for level in range(1, SWEEPS):
        sweep(level, level + 1, 8 + level, edges=True)

    send2 = send.reshape(STEPS * ROWS, COLS)
    middle = pl.ds(PAD + 8, 64)

    def rows64(i):
        return pl.ds(i * 64, 64)

    for i in range(8):
        high, low = halves(jnp.concatenate([fr[-1][8 + i, middle, :], fi[-1][8 + i, middle, :]], 1))
        lhs[rows64(i), :] = jnp.concatenate([high, low, high], 1)

    back[...] = jnp.dot(lhs[...], inv[...], preferred_element_type=F32)

    for i in range(8):
        both = back[rows64(i), :]
        both = jnp.concatenate([both[:, :128], both[:, 128:]], 0).T
        send2[pl.ds(i, STEPS, stride=ROWS), :] = both[:STEPS]
        send2[pl.ds(15 - i, STEPS, stride=ROWS), :] = both[STEPS:]

    def leaving(p):
        return pltpu.make_async_remote_copy(
            src_ref=send.at[p],
            dst_ref=out.at[rows16(zl), tile(col)],
            send_sem=out_send, recv_sem=out_recv,
            device_id=(p, s), device_id_type=MESH,
        )

    @pl.loop(1, STEPS)
    def _(d):
        leaving((t + d) % STEPS).start()

    mine = pltpu.make_async_copy(send.at[t], out.at[rows16(zl), tile(col)], mine_sem)
    mine.start()
    blocks(STEPS - 1, in_send, out_recv).wait_send()
    blocks(STEPS - 1, out_send, out_recv).wait_send()
    blocks(STEPS - 1, out_send, out_recv).wait_recv()
    mine.wait()


def per_device(source, diffusivity):
    dma = pltpu.SemaphoreType.DMA

    def vmem(*shape):
        return pltpu.VMEM(shape, F32)

    level = vmem(FOLD + 1, WIDE + 2 * PAD, 128)
    plane = vmem(FOLD, WIDE, 128)
    edge = vmem(FOLD, 8, 128)
    result = pl.pallas_call(
        body,
        out_shape=jax.ShapeDtypeStruct(source.shape[1:], F32),
        in_specs=[pl.BlockSpec(memory_space=pl.ANY)] * 2,
        out_specs=pl.BlockSpec(memory_space=pl.ANY),
        scratch_shapes=[
            pltpu.VMEM((768, 256), BF16), pltpu.VMEM((768, 256), BF16), vmem(512, 256),
            vmem(STEPS, ROWS, COLS), vmem(STEPS, 8, COLS), vmem(STEPS, 8, COLS),
            vmem(8, 3 * COLS), vmem(24, 3 * COLS), vmem(3 * COLS, 128),
            level, vmem(FOLD + 1, WIDE, 128), plane, plane, plane, plane, plane,
            pltpu.VMEM((512, 768), BF16), plane, plane, edge, edge, edge, edge,
            vmem(STEPS, ROWS, COLS),
        ]
        + [level] * (2 * SWEEPS)
        + [
            dma, dma((4,)), dma((4, 2)), dma((4, 2)), dma((3,)), dma((3,)), dma((2, 2)), dma((2, 2)),
            dma, dma, dma((3,)), dma,
        ],
        compiler_params=pltpu.CompilerParams(
            collective_id=0, has_side_effects=True, vmem_limit_bytes=56 * 2**20
        ),
        cost_estimate=pl.CostEstimate(flops=10**8, bytes_accessed=2**21, transcendentals=0),
    )(source[0], diffusivity)
    return result[None]


def solution(mesh):
    return jax.shard_map(
        per_device,
        mesh=mesh,
        in_specs=(P("tm", "space", None), P("space", None)),
        out_specs=P("tm", "space", None),
        check_vma=False,
    )
```

```python
import math

import jax
import jax.numpy as jnp
from jax import lax
from jax.experimental import pallas as pl
from jax.experimental.pallas import tpu as pltpu
from jax.sharding import PartitionSpec as P

SWEEPS = 8
STEPS = 64
circulant_alpha = 0.01
step_ratio = 4.0
damping = 0.8

MESH = pl.DeviceIdType.MESH
F32 = jnp.float32
BF16 = jnp.bfloat16
ROWS = 16
COLS = 128
HALF = STEPS // 2
FOLD = 16
WIDE = 80
PAD = 8
INNER = pl.ds(PAD, WIDE)


def iota(shape, axis):
    return lax.broadcasted_iota(jnp.int32, shape, axis)


def wave(steps, freq, imaginary):
    turn = jnp.where(imaginary, jnp.where(freq == 0, HALF * steps, steps * freq + STEPS // 4), steps * freq)
    return jnp.cos((turn % STEPS).astype(F32) * (2.0 * math.pi / STEPS))


def power(steps, sign):
    return jnp.exp(steps.astype(F32) * (sign * math.log(circulant_alpha) / STEPS))


def fill_forward(ref):
    shape = (STEPS, 8 * HALF)
    lane = iota(shape, 1)
    steps = iota(shape, 0)
    table = wave(steps, lane % HALF, lane >= 4 * HALF) * power(steps, 1.0) * (1.0 / step_ratio)
    for block in range(4):
        mine = (lane // HALF) % 4 == (block % 2) * 2 + block // 2
        high, low = halves(jnp.where(mine, table, 0.0))
        for base, value in ((0, high), (256, high), (512, low)):
            ref[pl.ds(base + block * STEPS, STEPS), :] = value


def fill_inverse(ref):
    shape = (4 * HALF, 4 * STEPS)
    row = iota(shape, 0)
    lane = iota(shape, 1)
    freq, steps, block = row % HALF, lane % STEPS, lane // STEPS
    mine = row // HALF == (block % 2) * 2 + block // 2
    scale = power(steps, -1.0) * jnp.where(mine, jnp.where(freq == 0, 1.0, 2.0) / STEPS, 0.0)
    for plane in range(2):
        high, low = halves(wave(steps, freq, plane == 1) * scale)
        for base, value in ((0, high), (256, high), (512, low)):
            ref[pl.ds(base + plane * 128, 128), :] = value


def offsets():
    every = [(y, z, x, c) for y in range(4) for z in range(2) for x in range(4) for c in range(2)]
    return sorted(every[1:], key=lambda o: -(min(o[0], 4 - o[0]) + o[1] + min(o[2], 4 - o[2])))


FARTHEST = offsets()


def place(t):
    return t // 16, (t // 8) % 2, (t // 2) % 4, t % 2


def column_of(t):
    y, _, x, core = place(t)
    along = x + (y % 2) * (3 - 2 * x)
    return (y * 4 + along) * 2 + core


def device_of(column, zl):
    y = column // 8
    along = (column // 2) % 4
    x = along + (y % 2) * (3 - 2 * along)
    return y * 16 + zl * 8 + x * 2 + column % 2


def part_of(value):
    return (lax.broadcasted_iota(jnp.int32, value.shape, value.ndim - 1) // 32) % 2


def swap_parts(value):
    axis = value.ndim - 1
    return jnp.where(part_of(value) == 0, pltpu.roll(value, 96, axis), pltpu.roll(value, 32, axis))


def halves(value):
    high = value.astype(BF16)
    low = (value - high.astype(F32)).astype(BF16)
    return high, low


def body(src, dif, out, *refs):
    (fwd, inv, back, recv, top, bottom, kap, knear, kwide, kfold, plink, qplus, qminus,
     gr, gs, gi, lhs, sr, si, pack_l, pack_r, got_l, got_r, send) = refs[:24]
    fr, fi = refs[24 : 24 + SWEEPS], refs[24 + SWEEPS : 24 + 2 * SWEEPS]
    (in_send, in_recv, z_send, z_recv, k_send, k_recv, c_send, c_recv, out_send, out_recv,
     near_sem, mine_sem) = refs[24 + 2 * SWEEPS :]
    t = lax.axis_index("tm")
    s = lax.axis_index("space")
    y, zl, x, core = place(t)
    col = column_of(t)
    z = s * 2 + zl

    def z_device(step):
        other = (z + step + 8) % 8
        return (t + (other % 2 - zl) * 8, other // 2)

    outer = z_device(2 * zl - 1)

    def tile(index):
        return pl.ds(pl.multiple_of(index * COLS, COLS), COLS)

    def rows16(index):
        return pl.ds(pl.multiple_of(index * ROWS, ROWS), ROWS)

    barrier = pltpu.get_barrier_semaphore()

    for dy, dz, dx, dc in FARTHEST:
        there = ((y + dy) % 4) * 16 + ((zl + dz) % 2) * 8 + ((x + dx) % 4) * 2 + (core + dc) % 2
        pl.semaphore_signal(barrier, inc=1, device_id=(there, s), device_id_type=MESH)

    above, below = z > 0, z < 7
    has_outer = above & below

    @pl.when(has_outer)
    def _():
        pl.semaphore_signal(barrier, inc=1, device_id=outer, device_id_type=MESH)

    loads = [
        pltpu.make_async_copy(
            dif.at[pl.ds(pl.multiple_of(zl * 8, 8), 24), tile((col + 31 + d) % 32)],
            knear.at[:, pl.ds(d * COLS, COLS)],
            near_sem.at[d],
        )
        for d in range(3)
    ]
    for c in loads:
        c.start()
    pl.semaphore_wait(barrier, STEPS - 1 + has_outer.astype(jnp.int32))

    def arriving(p):
        _, pzl, _, _ = place(p)
        return pltpu.make_async_remote_copy(
            src_ref=src.at[rows16(pzl), tile(column_of(p))],
            dst_ref=recv.at[t],
            send_sem=in_send, recv_sem=in_recv.at[y],
            device_id=(p, s), device_id_type=MESH,
        )

    krow = pl.ds(pl.multiple_of(zl * 24, 8), 8)
    kcopies = [
        pltpu.make_async_remote_copy(
            src_ref=dif.at[krow, tile((col + 31 + d) % 32)],
            dst_ref=kap.at[:, pl.ds(d * COLS, COLS)],
            send_sem=k_send.at[d], recv_sem=k_recv.at[d],
            device_id=outer, device_id_type=MESH,
        )
        for d in range(3)
    ]
    @pl.when(has_outer)
    def _():
        for c in kcopies:
            c.start()


    @pl.loop(1, STEPS)
    def _(d):
        arriving((t + d) % STEPS).start()

    own = pltpu.make_async_copy(src.at[rows16(zl), tile(col)], recv.at[t], in_recv.at[y])
    own.start()

    def blocks(count, send_sem, recv_sem):
        some = recv.at[pl.ds(0, count)]
        return pltpu.make_async_remote_copy(
            src_ref=some, dst_ref=some, send_sem=send_sem, recv_sem=recv_sem,
            device_id=outer, device_id_type=MESH,
        )

    def link(j):
        here = kfold[j, INNER, :]
        south = 0.5 * (here + kfold[j + 1, INNER, :])
        east = 0.5 * (here + kfold[j, pl.ds(PAD + 1, WIDE), :])
        west = 0.5 * (here + kfold[j, pl.ds(PAD - 1, WIDE), :])
        plink[j + 1] = south
        qplus[j] = east
        qminus[j] = west
        total = step_ratio * (plink[j] + south + east + west)
        inside = jnp.where(here > 0.0, damping * step_ratio, 0.0)
        diag = lam_re + total
        scale = inside / (diag * diag + lam_im * lam_im)
        gr[j] = scale * diag
        gi[j] = scale * lam_im
        diag = lam_other + total
        gs[j] = inside * diag / (diag * diag + lam_im * lam_im)

    def gather_coefficients():
        for c in loads:
            c.wait()
        @pl.when(has_outer)
        def _():
            for c in kcopies:
                c.wait()

        row_id = lax.broadcasted_iota(jnp.int32, (32, COLS), 0)
        low_ok = jnp.where(z > 0, 0, 8)
        high_ok = jnp.where(z < 7, 32, 24)
        for d in range(3):
            near24 = knear[:, d * COLS : (d + 1) * COLS]
            far8 = kap[:, d * COLS : (d + 1) * COLS]
            strip = jnp.where(
                zl == 0, jnp.concatenate([far8, near24], 0), jnp.concatenate([near24, far8], 0)
            )
            keep = (row_id >= low_ok) & (row_id < high_ok)
            if d == 0:
                keep = keep & (col > 0)
            if d == 2:
                keep = keep & (col < 31)
            strip = jnp.where(keep, strip, 0.0)
            strip = jnp.concatenate([strip, jnp.zeros((96, COLS), F32)], 0)
            kwide[pl.ds(d * COLS, COLS), :] = strip.T
        for at in (pl.ds(0, PAD), pl.ds(PAD + WIDE, PAD)):
            kfold[:, at, :] = jnp.zeros((FOLD + 1, PAD, 128), F32)
        lane = lax.broadcasted_iota(jnp.int32, (WIDE, 128), 1)
        is_a = lane < 64
        is_0 = lane % 64 < 32
        part0 = kwide[pl.ds(COLS - 8, WIDE), :]
        part1 = kwide[pl.ds(COLS + 56, WIDE), :]
        for j in range(FOLD):
            k = 31 - j
            kfold[j, INNER, :] = jnp.where(
                is_a,
                jnp.where(is_0, part0[:, j : j + 1], part1[:, j : j + 1]),
                jnp.where(is_0, part0[:, k : k + 1], part1[:, k : k + 1]),
            )
        kfold[FOLD, INNER, :] = pltpu.roll(kfold[FOLD - 1, INNER, :], 64, 1)

    def clear_edges():
        for missing, ref in ((z == 0, top), (z == 7, bottom)):

            @pl.when(missing)
            def _():
                ref[...] = jnp.zeros(ref.shape, F32)

        edge = jnp.zeros((FOLD + 1, PAD, 128), F32)
        for ref in fr[:-1] + fi[:-1]:
            ref[:, pl.ds(0, PAD), :] = edge
            ref[:, pl.ds(PAD + WIDE, PAD), :] = edge

    slot = iota((1, 128), 1) % HALF
    root = circulant_alpha ** (1.0 / STEPS)
    theta = slot.astype(F32) * (2.0 * math.pi / STEPS)
    lam_re = 1.0 - root * jnp.cos(theta)
    lam_im = root * jnp.sin(theta)
    lam_other = jnp.where(slot == 0, 1.0 + root, lam_re)


    def links(first, last):
        @pl.loop(first, last)
        def _(j):
            link(j)

    def prepare(phase):
        if phase == 0:
            gather_coefficients()
            plink[0] = kfold[0, INNER, :]
        elif phase == 1:
            links(0, 8)
        elif phase == 2:
            links(8, FOLD)
        else:
            clear_edges()
            fill_forward(fwd)

    zcopies = []
    for phase in range(4):
        prepare(phase)
        group = (y + 3 - phase) % 4
        blocks(16, in_send, in_recv.at[group]).wait_recv()
        steps = pl.ds(group * 16, 16)
        pair = [
            pltpu.make_async_remote_copy(
                src_ref=recv.at[steps, pl.ds(0, 8), :], dst_ref=bottom.at[steps],
                send_sem=z_send.at[phase, 0], recv_sem=z_recv.at[phase, 0],
                device_id=z_device(-1), device_id_type=MESH,
            ),
            pltpu.make_async_remote_copy(
                src_ref=recv.at[steps, pl.ds(8, 8), :], dst_ref=top.at[steps],
                send_sem=z_send.at[phase, 1], recv_sem=z_recv.at[phase, 1],
                device_id=z_device(1), device_id_type=MESH,
            ),
        ]
        zcopies.append(pair)
        pl.when(above)(pair[0].start)
        pl.when(below)(pair[1].start)

    left = device_of((col + 31) % 32, zl)
    right = device_of((col + 1) % 32, zl)

    def fold_in(i, first, second):
        high, low = halves(jnp.concatenate([first, second], 0).T)
        pieces = [high[:64], high[64:], low[:64], low[64:], high[:64], high[64:]]
        lhs[pl.ds(i * 64, 64), :] = jnp.concatenate(pieces, 1)

    def transformed(start, stage):
        result = jnp.dot(lhs[...], fwd[...], preferred_element_type=F32)
        sr[pl.ds(start, 8), pl.ds(8, 64), :] = result[:, :128].reshape(8, 64, 128)
        si[pl.ds(start, 8), pl.ds(8, 64), :] = result[:, 128:].reshape(8, 64, 128)
        mine = pl.ds(start, 8)
        re, im = sr[mine, pl.ds(8, 8), :], si[mine, pl.ds(8, 8), :]
        pack_l[mine] = jnp.where(part_of(re) == 0, re, swap_parts(im))
        re, im = sr[mine, pl.ds(64, 8), :], si[mine, pl.ds(64, 8), :]
        pack_r[mine] = jnp.where(part_of(re) == 1, re, swap_parts(im))
        copies = [
            pltpu.make_async_remote_copy(
                src_ref=pack_l.at[mine], dst_ref=got_r.at[mine],
                send_sem=c_send.at[stage, 0], recv_sem=c_recv.at[stage, 0],
                device_id=(left, s), device_id_type=MESH,
            ),
            pltpu.make_async_remote_copy(
                src_ref=pack_r.at[mine], dst_ref=got_l.at[mine],
                send_sem=c_send.at[stage, 1], recv_sem=c_recv.at[stage, 1],
                device_id=(right, s), device_id_type=MESH,
            ),
        ]
        for c in copies:
            c.start()
        return copies

    def join(j, from_left, from_right):
        re, im = sr[j, pl.ds(64, 8), :], si[j, pl.ds(64, 8), :]
        part = part_of(re)
        sr[j, pl.ds(0, 8), :] = swap_parts(jnp.where(part == 1, from_left, re))
        si[j, pl.ds(0, 8), :] = jnp.where(part == 0, from_left, swap_parts(im))
        re, im = sr[j, pl.ds(8, 8), :], si[j, pl.ds(8, 8), :]
        sr[j, pl.ds(72, 8), :] = swap_parts(jnp.where(part == 0, from_right, re))
        si[j, pl.ds(72, 8), :] = jnp.where(part == 1, from_right, swap_parts(im))

    def first_level(j, start, size):
        at = pl.ds(start, size)
        re, im, cross = sr[j, at, :], si[j, at, :], gi[j, at, :]
        fr[0][j, pl.ds(PAD + start, size), :] = gr[j, at, :] * re + cross * im
        fi[0][j, pl.ds(PAD + start, size), :] = gs[j, at, :] * im - cross * re

    def seam(level):
        for ref in (fr[level], fi[level]):
            ref[FOLD, INNER, :] = pltpu.roll(ref[FOLD - 1, INNER, :], 64, 1)

    def sweep(level, first, last, edges=False):
        pr, pi, nr, ni = fr[level - 1], fi[level - 1], fr[level], fi[level]
        if level == SWEEPS - 1:
            spans = ((8, 8), (64, 8)) if edges else ((8, 32), (40, 32))
        else:
            spans = ((0, 16), (64, 16)) if edges else ((0, 40), (40, 40))

        @pl.loop(first, last, unroll=7 if edges else (last - first if first >= 9 else 7))
        def _(j):
            for start, size in spans:
                at, mid = pl.ds(start, size), pl.ds(PAD + start, size)
                west, east = pl.ds(PAD - 1 + start, size), pl.ds(PAD + 1 + start, size)
                p0, p1, q0, q1 = plink[j, at, :], plink[j + 1, at, :], qminus[j, at, :], qplus[j, at, :]
                vr = sr[j, at, :] + p0 * pr[j - 1, mid, :] + p1 * pr[j + 1, mid, :]
                vr = vr + (q0 * pr[j, west, :] + q1 * pr[j, east, :])
                vi = si[j, at, :] + p0 * pi[j - 1, mid, :] + p1 * pi[j + 1, mid, :]
                vi = vi + (q0 * pi[j, west, :] + q1 * pi[j, east, :])
                cross = gi[j, at, :]
                nr[j, mid, :] = (1.0 - damping) * pr[j, mid, :] + (gr[j, at, :] * vr + cross * vi)
                ni[j, mid, :] = (1.0 - damping) * pi[j, mid, :] + (gs[j, at, :] * vi - cross * vr)

    recv2 = recv.reshape(STEPS * ROWS, COLS)

    for i in range(8):
        fold_in(i, recv2[pl.ds(i, STEPS, stride=ROWS), :], recv2[pl.ds(15 - i, STEPS, stride=ROWS), :])

    inside = transformed(8, 0)
    fill_inverse(inv)
    for c in inside:
        c.wait()

    @pl.loop(8, FOLD)
    def _(j):
        join(j, got_l[j], got_r[j])
        first_level(j, 0, WIDE)

    seam(0)
    for level in range(1, SWEEPS):
        sweep(level, 8 + level, FOLD)
        if level < SWEEPS - 1:
            seam(level)

    for up, down in zcopies:

        @pl.when(above)
        def _():
            up.wait_send()
            down.wait_recv()

        @pl.when(below)
        def _():
            down.wait_send()
            up.wait_recv()

    top2 = top.reshape(STEPS * 8, COLS)
    bottom2 = bottom.reshape(STEPS * 8, COLS)

    for h in range(8):
        fold_in(h, top2[pl.ds(h, STEPS, stride=8), :], bottom2[pl.ds(7 - h, STEPS, stride=8), :])

    outside = transformed(0, 1)

    @pl.loop(0, 8, unroll=8)
    def _(j):
        nothing = jnp.zeros((8, 128), F32)
        join(j, nothing, nothing)
        first_level(j, 0, WIDE)

    for level in range(1, SWEEPS):
        sweep(level, level + 1, 8 + level)
    for c in outside:
        c.wait()

    @pl.loop(0, 8, unroll=8)
    def _(j):
        join(j, got_l[j], got_r[j])
        first_level(j, 0, 16)
        first_level(j, 64, 16)

    for level in range(1, SWEEPS):
        sweep(level, level + 1, 8 + level, edges=True)

    send2 = send.reshape(STEPS * ROWS, COLS)
    middle = pl.ds(PAD + 8, 64)

    def rows64(i):
        return pl.ds(i * 64, 64)

    for i in range(8):
        high, low = halves(jnp.concatenate([fr[-1][8 + i, middle, :], fi[-1][8 + i, middle, :]], 1))
        lhs[rows64(i), :] = jnp.concatenate([high, low, high], 1)

    back[...] = jnp.dot(lhs[...], inv[...], preferred_element_type=F32)

    for i in range(8):
        both = back[rows64(i), :]
        both = jnp.concatenate([both[:, :128], both[:, 128:]], 0).T
        send2[pl.ds(i, STEPS, stride=ROWS), :] = both[:STEPS]
        send2[pl.ds(15 - i, STEPS, stride=ROWS), :] = both[STEPS:]

    def leaving(p):
        return pltpu.make_async_remote_copy(
            src_ref=send.at[p],
            dst_ref=out.at[rows16(zl), tile(col)],
            send_sem=out_send, recv_sem=out_recv,
            device_id=(p, s), device_id_type=MESH,
        )

    @pl.loop(1, STEPS)
    def _(d):
        leaving((t + d) % STEPS).start()

    mine = pltpu.make_async_copy(send.at[t], out.at[rows16(zl), tile(col)], mine_sem)
    mine.start()
    blocks(STEPS - 1, in_send, out_recv).wait_send()
    blocks(STEPS - 1, out_send, out_recv).wait_send()
    blocks(STEPS - 1, out_send, out_recv).wait_recv()
    mine.wait()


def per_device(source, diffusivity):
    dma = pltpu.SemaphoreType.DMA

    def vmem(*shape):
        return pltpu.VMEM(shape, F32)

    level = vmem(FOLD + 1, WIDE + 2 * PAD, 128)
    plane = vmem(FOLD, WIDE, 128)
    edge = vmem(FOLD, 8, 128)
    result = pl.pallas_call(
        body,
        out_shape=jax.ShapeDtypeStruct(source.shape[1:], F32),
        in_specs=[pl.BlockSpec(memory_space=pl.ANY)] * 2,
        out_specs=pl.BlockSpec(memory_space=pl.ANY),
        scratch_shapes=[
            pltpu.VMEM((768, 256), BF16), pltpu.VMEM((768, 256), BF16), vmem(512, 256),
            vmem(STEPS, ROWS, COLS), vmem(STEPS, 8, COLS), vmem(STEPS, 8, COLS),
            vmem(8, 3 * COLS), vmem(24, 3 * COLS), vmem(3 * COLS, 128),
            level, vmem(FOLD + 1, WIDE, 128), plane, plane, plane, plane, plane,
            pltpu.VMEM((512, 768), BF16), plane, plane, edge, edge, edge, edge,
            vmem(STEPS, ROWS, COLS),
        ]
        + [level] * (2 * SWEEPS)
        + [
            dma, dma((4,)), dma((4, 2)), dma((4, 2)), dma((3,)), dma((3,)), dma((2, 2)), dma((2, 2)),
            dma, dma, dma((3,)), dma,
        ],
        compiler_params=pltpu.CompilerParams(
            collective_id=0, has_side_effects=True, vmem_limit_bytes=425 * 2**17
        ),
        cost_estimate=pl.CostEstimate(flops=10**8, bytes_accessed=2**21, transcendentals=0),
    )(source[0], diffusivity)
    return result[None]


def solution(mesh):
    return jax.shard_map(
        per_device,
        mesh=mesh,
        in_specs=(P("tm", "space", None), P("space", None)),
        out_specs=P("tm", "space", None),
        check_vma=False,
    )
```

```python
import math

import jax
import jax.numpy as jnp
from jax import lax
from jax.experimental import pallas as pl
from jax.experimental.pallas import tpu as pltpu
from jax.sharding import PartitionSpec as P

SWEEPS = 8
STEPS = 64
circulant_alpha = 0.01
step_ratio = 4.0
damping = 0.8

MESH = pl.DeviceIdType.MESH
F32 = jnp.float32
BF16 = jnp.bfloat16
ROWS = 16
COLS = 128
HALF = STEPS // 2
FOLD = 16
WIDE = 80
PAD = 8
INNER = pl.ds(PAD, WIDE)


def iota(shape, axis):
    return lax.broadcasted_iota(jnp.int32, shape, axis)


def wave(steps, freq, imaginary):
    turn = jnp.where(imaginary, jnp.where(freq == 0, HALF * steps, steps * freq + STEPS // 4), steps * freq)
    return jnp.cos((turn % STEPS).astype(F32) * (2.0 * math.pi / STEPS))


def power(steps, sign):
    return jnp.exp(steps.astype(F32) * (sign * math.log(circulant_alpha) / STEPS))


def fill_forward(ref):
    shape = (STEPS, 8 * HALF)
    lane = iota(shape, 1)
    steps = iota(shape, 0)
    table = wave(steps, lane % HALF, lane >= 4 * HALF) * power(steps, 1.0) * (1.0 / step_ratio)
    for block in range(4):
        mine = (lane // HALF) % 4 == (block % 2) * 2 + block // 2
        high, low = halves(jnp.where(mine, table, 0.0))
        for base, value in ((0, high), (256, high), (512, low)):
            ref[pl.ds(base + block * STEPS, STEPS), :] = value


def fill_inverse(ref):
    shape = (4 * HALF, 4 * STEPS)
    row = iota(shape, 0)
    lane = iota(shape, 1)
    freq, steps, block = row % HALF, lane % STEPS, lane // STEPS
    mine = row // HALF == (block % 2) * 2 + block // 2
    scale = power(steps, -1.0) * jnp.where(mine, jnp.where(freq == 0, 1.0, 2.0) / STEPS, 0.0)
    for plane in range(2):
        high, low = halves(wave(steps, freq, plane == 1) * scale)
        for base, value in ((0, high), (256, high), (512, low)):
            ref[pl.ds(base + plane * 128, 128), :] = value


def offsets():
    every = [(y, z, x, c) for y in range(4) for z in range(2) for x in range(4) for c in range(2)]
    return sorted(every[1:], key=lambda o: -(min(o[0], 4 - o[0]) + o[1] + min(o[2], 4 - o[2])))


FARTHEST = offsets()
GREETED = [o for o in FARTHEST if o[1] == 0 or sum(o) == 1]


def place(t):
    return t // 16, (t // 8) % 2, (t // 2) % 4, t % 2


def column_of(t):
    y, _, x, core = place(t)
    along = x + (y % 2) * (3 - 2 * x)
    return (y * 4 + along) * 2 + core


def device_of(column, zl):
    y = column // 8
    along = (column // 2) % 4
    x = along + (y % 2) * (3 - 2 * along)
    return y * 16 + zl * 8 + x * 2 + column % 2


def part_of(value):
    return (lax.broadcasted_iota(jnp.int32, value.shape, value.ndim - 1) // 32) % 2


def swap_parts(value):
    axis = value.ndim - 1
    return jnp.where(part_of(value) == 0, pltpu.roll(value, 96, axis), pltpu.roll(value, 32, axis))


def halves(value):
    high = value.astype(BF16)
    low = (value - high.astype(F32)).astype(BF16)
    return high, low


def body(src, dif, out, *refs):
    (fwd, inv, back, recv, top, bottom, kap, knear, kwide, kfold, plink, qplus, qminus,
     gr, gs, gi, lhs, sr, si, pack_l, pack_r, got_l, got_r, send) = refs[:24]
    fr, fi = refs[24 : 24 + SWEEPS], refs[24 + SWEEPS : 24 + 2 * SWEEPS]
    (in_send, in_recv, z_send, z_recv, k_send, k_recv, c_send, c_recv, out_send, out_recv,
     near_sem, mine_sem, plane_sem) = refs[24 + 2 * SWEEPS :]
    t = lax.axis_index("tm")
    s = lax.axis_index("space")
    y, zl, x, core = place(t)
    col = column_of(t)
    z = s * 2 + zl

    def z_device(step):
        other = (z + step + 8) % 8
        return (t + (other % 2 - zl) * 8, other // 2)

    outer = z_device(2 * zl - 1)

    def tile(index):
        return pl.ds(pl.multiple_of(index * COLS, COLS), COLS)

    def rows16(index):
        return pl.ds(pl.multiple_of(index * ROWS, ROWS), ROWS)

    barrier = pltpu.get_barrier_semaphore()

    for dy, dz, dx, dc in GREETED:
        there = ((y + dy) % 4) * 16 + ((zl + dz) % 2) * 8 + ((x + dx) % 4) * 2 + (core + dc) % 2
        pl.semaphore_signal(barrier, inc=1, device_id=(there, s), device_id_type=MESH)

    above, below = z > 0, z < 7
    has_outer = above & below

    @pl.when(has_outer)
    def _():
        pl.semaphore_signal(barrier, inc=1, device_id=outer, device_id_type=MESH)

    loads = [
        pltpu.make_async_copy(
            dif.at[pl.ds(pl.multiple_of(zl * 8, 8), 24), tile((col + 31 + d) % 32)],
            knear.at[:, pl.ds(d * COLS, COLS)],
            near_sem.at[d],
        )
        for d in range(3)
    ]
    for c in loads:
        c.start()
    pl.semaphore_wait(barrier, STEPS // 2 + has_outer.astype(jnp.int32))
    pl.semaphore_signal(
        plane_sem, inc=1, device_id=(t + 8 - 16 * zl, s), device_id_type=MESH
    )

    def arriving(p):
        _, pzl, _, _ = place(p)
        return pltpu.make_async_remote_copy(
            src_ref=src.at[rows16(pzl), tile(column_of(p))],
            dst_ref=recv.at[t],
            send_sem=in_send, recv_sem=in_recv.at[t // 8],
            device_id=(p, s), device_id_type=MESH,
        )

    krow = pl.ds(pl.multiple_of(zl * 24, 8), 8)
    kcopies = [
        pltpu.make_async_remote_copy(
            src_ref=dif.at[krow, tile((col + 31 + d) % 32)],
            dst_ref=kap.at[:, pl.ds(d * COLS, COLS)],
            send_sem=k_send.at[d], recv_sem=k_recv.at[d],
            device_id=outer, device_id_type=MESH,
        )
        for d in range(3)
    ]
    @pl.when(has_outer)
    def _():
        for c in kcopies:
            c.start()


    def in_plane(d, plane):
        turned = (y * 8 + x * 2 + core + d) % 32
        return (turned // 8) * 16 + plane * 8 + turned % 8

    @pl.loop(1, STEPS // 2)
    def _(d):
        arriving(in_plane(d, zl)).start()

    pl.semaphore_wait(plane_sem, 1)

    @pl.loop(0, STEPS // 2)
    def _(d):
        arriving(in_plane(d, 1 - zl)).start()

    own = pltpu.make_async_copy(src.at[rows16(zl), tile(col)], recv.at[t], in_recv.at[t // 8])
    own.start()

    def blocks(count, send_sem, recv_sem):
        some = recv.at[pl.ds(0, count)]
        return pltpu.make_async_remote_copy(
            src_ref=some, dst_ref=some, send_sem=send_sem, recv_sem=recv_sem,
            device_id=outer, device_id_type=MESH,
        )

    def link(j):
        here = kfold[j, INNER, :]
        south = 0.5 * (here + kfold[j + 1, INNER, :])
        east = 0.5 * (here + kfold[j, pl.ds(PAD + 1, WIDE), :])
        west = 0.5 * (here + kfold[j, pl.ds(PAD - 1, WIDE), :])
        plink[j + 1] = south
        qplus[j] = east
        qminus[j] = west
        total = step_ratio * (plink[j] + south + east + west)
        inside = jnp.where(here > 0.0, damping * step_ratio, 0.0)
        diag = lam_re + total
        scale = inside / (diag * diag + lam_im * lam_im)
        gr[j] = scale * diag
        gi[j] = scale * lam_im
        diag = lam_other + total
        gs[j] = inside * diag / (diag * diag + lam_im * lam_im)

    def gather_coefficients():
        for c in loads:
            c.wait()
        @pl.when(has_outer)
        def _():
            for c in kcopies:
                c.wait()

        row_id = lax.broadcasted_iota(jnp.int32, (32, COLS), 0)
        low_ok = jnp.where(z > 0, 0, 8)
        high_ok = jnp.where(z < 7, 32, 24)
        for d in range(3):
            near24 = knear[:, d * COLS : (d + 1) * COLS]
            far8 = kap[:, d * COLS : (d + 1) * COLS]
            strip = jnp.where(
                zl == 0, jnp.concatenate([far8, near24], 0), jnp.concatenate([near24, far8], 0)
            )
            keep = (row_id >= low_ok) & (row_id < high_ok)
            if d == 0:
                keep = keep & (col > 0)
            if d == 2:
                keep = keep & (col < 31)
            strip = jnp.where(keep, strip, 0.0)
            strip = jnp.concatenate([strip, jnp.zeros((96, COLS), F32)], 0)
            kwide[pl.ds(d * COLS, COLS), :] = strip.T
        for at in (pl.ds(0, PAD), pl.ds(PAD + WIDE, PAD)):
            kfold[:, at, :] = jnp.zeros((FOLD + 1, PAD, 128), F32)
        lane = lax.broadcasted_iota(jnp.int32, (WIDE, 128), 1)
        is_a = lane < 64
        is_0 = lane % 64 < 32
        part0 = kwide[pl.ds(COLS - 8, WIDE), :]
        part1 = kwide[pl.ds(COLS + 56, WIDE), :]
        for j in range(FOLD):
            k = 31 - j
            kfold[j, INNER, :] = jnp.where(
                is_a,
                jnp.where(is_0, part0[:, j : j + 1], part1[:, j : j + 1]),
                jnp.where(is_0, part0[:, k : k + 1], part1[:, k : k + 1]),
            )
        kfold[FOLD, INNER, :] = pltpu.roll(kfold[FOLD - 1, INNER, :], 64, 1)

    def clear_edges():
        for missing, ref in ((z == 0, top), (z == 7, bottom)):

            @pl.when(missing)
            def _():
                ref[...] = jnp.zeros(ref.shape, F32)

        edge = jnp.zeros((FOLD + 1, PAD, 128), F32)
        for ref in fr[:-1] + fi[:-1]:
            ref[:, pl.ds(0, PAD), :] = edge
            ref[:, pl.ds(PAD + WIDE, PAD), :] = edge

    slot = iota((1, 128), 1) % HALF
    root = circulant_alpha ** (1.0 / STEPS)
    theta = slot.astype(F32) * (2.0 * math.pi / STEPS)
    lam_re = 1.0 - root * jnp.cos(theta)
    lam_im = root * jnp.sin(theta)
    lam_other = jnp.where(slot == 0, 1.0 + root, lam_re)


    def links(first, last):
        @pl.loop(first, last)
        def _(j):
            link(j)

    def prepare(phase):
        if phase == 0:
            gather_coefficients()
            plink[0] = kfold[0, INNER, :]
        elif phase < 5:
            links(4 * phase - 4, 4 * phase)
        elif phase == 5:
            clear_edges()
        elif phase == 6:
            fill_forward(fwd)

    zcopies = []
    for phase in range(8):
        prepare(phase)
        group = ((y + 3 - phase % 4) % 4) * 2 + (zl + phase // 4) % 2
        blocks(8, in_send, in_recv.at[group]).wait_recv()
        steps = pl.ds(group * 8, 8)
        pair = [
            pltpu.make_async_remote_copy(
                src_ref=recv.at[steps, pl.ds(0, 8), :], dst_ref=bottom.at[steps],
                send_sem=z_send.at[phase, 0], recv_sem=z_recv.at[phase, 0],
                device_id=z_device(-1), device_id_type=MESH,
            ),
            pltpu.make_async_remote_copy(
                src_ref=recv.at[steps, pl.ds(8, 8), :], dst_ref=top.at[steps],
                send_sem=z_send.at[phase, 1], recv_sem=z_recv.at[phase, 1],
                device_id=z_device(1), device_id_type=MESH,
            ),
        ]
        zcopies.append(pair)
        pl.when(above)(pair[0].start)
        pl.when(below)(pair[1].start)

    left = device_of((col + 31) % 32, zl)
    right = device_of((col + 1) % 32, zl)

    def fold_in(i, first, second):
        high, low = halves(jnp.concatenate([first, second], 0).T)
        pieces = [high[:64], high[64:], low[:64], low[64:], high[:64], high[64:]]
        lhs[pl.ds(i * 64, 64), :] = jnp.concatenate(pieces, 1)

    def transformed(start, stage):
        result = jnp.dot(lhs[...], fwd[...], preferred_element_type=F32)
        sr[pl.ds(start, 8), pl.ds(8, 64), :] = result[:, :128].reshape(8, 64, 128)
        si[pl.ds(start, 8), pl.ds(8, 64), :] = result[:, 128:].reshape(8, 64, 128)
        mine = pl.ds(start, 8)
        re, im = sr[mine, pl.ds(8, 8), :], si[mine, pl.ds(8, 8), :]
        pack_l[mine] = jnp.where(part_of(re) == 0, re, swap_parts(im))
        re, im = sr[mine, pl.ds(64, 8), :], si[mine, pl.ds(64, 8), :]
        pack_r[mine] = jnp.where(part_of(re) == 1, re, swap_parts(im))
        copies = [
            pltpu.make_async_remote_copy(
                src_ref=pack_l.at[mine], dst_ref=got_r.at[mine],
                send_sem=c_send.at[stage, 0], recv_sem=c_recv.at[stage, 0],
                device_id=(left, s), device_id_type=MESH,
            ),
            pltpu.make_async_remote_copy(
                src_ref=pack_r.at[mine], dst_ref=got_l.at[mine],
                send_sem=c_send.at[stage, 1], recv_sem=c_recv.at[stage, 1],
                device_id=(right, s), device_id_type=MESH,
            ),
        ]
        for c in copies:
            c.start()
        return copies

    def join(j, from_left, from_right):
        re, im = sr[j, pl.ds(64, 8), :], si[j, pl.ds(64, 8), :]
        part = part_of(re)
        sr[j, pl.ds(0, 8), :] = swap_parts(jnp.where(part == 1, from_left, re))
        si[j, pl.ds(0, 8), :] = jnp.where(part == 0, from_left, swap_parts(im))
        re, im = sr[j, pl.ds(8, 8), :], si[j, pl.ds(8, 8), :]
        sr[j, pl.ds(72, 8), :] = swap_parts(jnp.where(part == 0, from_right, re))
        si[j, pl.ds(72, 8), :] = jnp.where(part == 1, from_right, swap_parts(im))

    def first_level(j, start, size):
        at = pl.ds(start, size)
        re, im, cross = sr[j, at, :], si[j, at, :], gi[j, at, :]
        fr[0][j, pl.ds(PAD + start, size), :] = gr[j, at, :] * re + cross * im
        fi[0][j, pl.ds(PAD + start, size), :] = gs[j, at, :] * im - cross * re

    def seam(level):
        for ref in (fr[level], fi[level]):
            ref[FOLD, INNER, :] = pltpu.roll(ref[FOLD - 1, INNER, :], 64, 1)

    def sweep(level, first, last, edges=False):
        pr, pi, nr, ni = fr[level - 1], fi[level - 1], fr[level], fi[level]
        if level == SWEEPS - 1:
            spans = ((8, 8), (64, 8)) if edges else ((8, 32), (40, 32))
        else:
            spans = ((0, 16), (64, 16)) if edges else ((0, 40), (40, 40))

        @pl.loop(first, last, unroll=7 if edges else (last - first if first >= 9 else 7))
        def _(j):
            for start, size in spans:
                at, mid = pl.ds(start, size), pl.ds(PAD + start, size)
                west, east = pl.ds(PAD - 1 + start, size), pl.ds(PAD + 1 + start, size)
                p0, p1, q0, q1 = plink[j, at, :], plink[j + 1, at, :], qminus[j, at, :], qplus[j, at, :]
                vr = sr[j, at, :] + p0 * pr[j - 1, mid, :] + p1 * pr[j + 1, mid, :]
                vr = vr + (q0 * pr[j, west, :] + q1 * pr[j, east, :])
                vi = si[j, at, :] + p0 * pi[j - 1, mid, :] + p1 * pi[j + 1, mid, :]
                vi = vi + (q0 * pi[j, west, :] + q1 * pi[j, east, :])
                cross = gi[j, at, :]
                nr[j, mid, :] = (1.0 - damping) * pr[j, mid, :] + (gr[j, at, :] * vr + cross * vi)
                ni[j, mid, :] = (1.0 - damping) * pi[j, mid, :] + (gs[j, at, :] * vi - cross * vr)

    recv2 = recv.reshape(STEPS * ROWS, COLS)

    for i in range(8):
        fold_in(i, recv2[pl.ds(i, STEPS, stride=ROWS), :], recv2[pl.ds(15 - i, STEPS, stride=ROWS), :])

    inside = transformed(8, 0)
    fill_inverse(inv)
    for c in inside:
        c.wait()

    @pl.loop(8, FOLD, unroll=8)
    def _(j):
        join(j, got_l[j], got_r[j])
        first_level(j, 0, WIDE)

    seam(0)
    for level in range(1, SWEEPS):
        sweep(level, 8 + level, FOLD)
        if level < SWEEPS - 1:
            seam(level)

    for up, down in zcopies:

        @pl.when(above)
        def _():
            up.wait_send()
            down.wait_recv()

        @pl.when(below)
        def _():
            down.wait_send()
            up.wait_recv()

    top2 = top.reshape(STEPS * 8, COLS)
    bottom2 = bottom.reshape(STEPS * 8, COLS)

    for h in range(8):
        fold_in(h, top2[pl.ds(h, STEPS, stride=8), :], bottom2[pl.ds(7 - h, STEPS, stride=8), :])

    outside = transformed(0, 1)

    @pl.loop(0, 8, unroll=8)
    def _(j):
        nothing = jnp.zeros((8, 128), F32)
        join(j, nothing, nothing)
        first_level(j, 0, WIDE)

    for level in range(1, SWEEPS):
        sweep(level, level + 1, 8 + level)
    for c in outside:
        c.wait()

    @pl.loop(0, 8, unroll=8)
    def _(j):
        join(j, got_l[j], got_r[j])
        first_level(j, 0, 16)
        first_level(j, 64, 16)

    for level in range(1, SWEEPS):
        sweep(level, level + 1, 8 + level, edges=True)

    send2 = send.reshape(STEPS * ROWS, COLS)
    middle = pl.ds(PAD + 8, 64)

    def rows64(i):
        return pl.ds(i * 64, 64)

    for i in range(8):
        high, low = halves(jnp.concatenate([fr[-1][8 + i, middle, :], fi[-1][8 + i, middle, :]], 1))
        lhs[rows64(i), :] = jnp.concatenate([high, low, high], 1)

    back[...] = jnp.dot(lhs[...], inv[...], preferred_element_type=F32)

    for i in range(8):
        both = back[rows64(i), :]
        both = jnp.concatenate([both[:, :128], both[:, 128:]], 0).T
        send2[pl.ds(i, STEPS, stride=ROWS), :] = both[:STEPS]
        send2[pl.ds(15 - i, STEPS, stride=ROWS), :] = both[STEPS:]

    def leaving(p):
        return pltpu.make_async_remote_copy(
            src_ref=send.at[p],
            dst_ref=out.at[rows16(zl), tile(col)],
            send_sem=out_send, recv_sem=out_recv,
            device_id=(p, s), device_id_type=MESH,
        )

    @pl.loop(1, STEPS)
    def _(d):
        leaving((t + d) % STEPS).start()

    mine = pltpu.make_async_copy(send.at[t], out.at[rows16(zl), tile(col)], mine_sem)
    mine.start()
    blocks(STEPS - 1, in_send, out_recv).wait_send()
    blocks(STEPS - 1, out_send, out_recv).wait_send()
    blocks(STEPS - 1, out_send, out_recv).wait_recv()
    mine.wait()


def per_device(source, diffusivity):
    dma = pltpu.SemaphoreType.DMA

    def vmem(*shape):
        return pltpu.VMEM(shape, F32)

    level = vmem(FOLD + 1, WIDE + 2 * PAD, 128)
    plane = vmem(FOLD, WIDE, 128)
    edge = vmem(FOLD, 8, 128)
    result = pl.pallas_call(
        body,
        out_shape=jax.ShapeDtypeStruct(source.shape[1:], F32),
        in_specs=[pl.BlockSpec(memory_space=pl.ANY)] * 2,
        out_specs=pl.BlockSpec(memory_space=pl.ANY),
        scratch_shapes=[
            pltpu.VMEM((768, 256), BF16), pltpu.VMEM((768, 256), BF16), vmem(512, 256),
            vmem(STEPS, ROWS, COLS), vmem(STEPS, 8, COLS), vmem(STEPS, 8, COLS),
            vmem(8, 3 * COLS), vmem(24, 3 * COLS), vmem(3 * COLS, 128),
            level, vmem(FOLD + 1, WIDE, 128), plane, plane, plane, plane, plane,
            pltpu.VMEM((512, 768), BF16), plane, plane, edge, edge, edge, edge,
            vmem(STEPS, ROWS, COLS),
        ]
        + [level] * (2 * SWEEPS)
        + [
            dma, dma((8,)), dma((8, 2)), dma((8, 2)), dma((3,)), dma((3,)), dma((2, 2)), dma((2, 2)),
            dma, dma, dma((3,)), dma, pltpu.SemaphoreType.REGULAR,
        ],
        compiler_params=pltpu.CompilerParams(
            collective_id=0, has_side_effects=True, vmem_limit_bytes=425 * 2**17
        ),
        cost_estimate=pl.CostEstimate(flops=10**8, bytes_accessed=2**21, transcendentals=0),
    )(source[0], diffusivity)
    return result[None]


def solution(mesh):
    return jax.shard_map(
        per_device,
        mesh=mesh,
        in_specs=(P("tm", "space", None), P("space", None)),
        out_specs=P("tm", "space", None),
        check_vma=False,
    )
```

```python
import math

import jax
import jax.numpy as jnp
from jax import lax
from jax.experimental import pallas as pl
from jax.experimental.pallas import tpu as pltpu
from jax.sharding import PartitionSpec as P

SWEEPS = 8
STEPS = 64
circulant_alpha = 0.01
step_ratio = 4.0
damping = 0.8

MESH = pl.DeviceIdType.MESH
F32 = jnp.float32
BF16 = jnp.bfloat16
ROWS = 16
COLS = 128
HALF = STEPS // 2
FOLD = 16
WIDE = 80
PAD = 8
PIECE = 4
INNER = pl.ds(PAD, WIDE)


def iota(shape, axis):
    return lax.broadcasted_iota(jnp.int32, shape, axis)


def wave(steps, freq, imaginary):
    turn = jnp.where(imaginary, jnp.where(freq == 0, HALF * steps, steps * freq + STEPS // 4), steps * freq)
    return jnp.cos((turn % STEPS).astype(F32) * (2.0 * math.pi / STEPS))


def power(steps, sign):
    return jnp.exp(steps.astype(F32) * (sign * math.log(circulant_alpha) / STEPS))


def fill_forward(ref):
    shape = (STEPS, 8 * HALF)
    lane = iota(shape, 1)
    steps = iota(shape, 0)
    table = wave(steps, lane % HALF, lane >= 4 * HALF) * power(steps, 1.0) * (1.0 / step_ratio)
    for block in range(4):
        mine = (lane // HALF) % 4 == (block % 2) * 2 + block // 2
        high, low = halves(jnp.where(mine, table, 0.0))
        for base, value in ((0, high), (256, high), (512, low)):
            ref[pl.ds(base + block * STEPS, STEPS), :] = value


def fill_inverse(ref):
    shape = (4 * HALF, 4 * STEPS)
    row = iota(shape, 0)
    lane = iota(shape, 1)
    freq, steps, block = row % HALF, lane % STEPS, lane // STEPS
    mine = row // HALF == (block % 2) * 2 + block // 2
    scale = power(steps, -1.0) * jnp.where(mine, jnp.where(freq == 0, 1.0, 2.0) / STEPS, 0.0)
    for plane in range(2):
        high, low = halves(wave(steps, freq, plane == 1) * scale)
        for base, value in ((0, high), (256, high), (512, low)):
            ref[pl.ds(base + plane * 128, 128), :] = value


def offsets():
    every = [(y, z, x, c) for y in range(4) for z in range(2) for x in range(4) for c in range(2)]
    return sorted(every[1:], key=lambda o: -(min(o[0], 4 - o[0]) + o[1] + min(o[2], 4 - o[2])))


FARTHEST = offsets()
GREETED = [o for o in FARTHEST if o[1] == 0 or sum(o) == 1]


def place(t):
    return t // 16, (t // 8) % 2, (t // 2) % 4, t % 2


def column_of(t):
    y, _, x, core = place(t)
    along = x + (y % 2) * (3 - 2 * x)
    return (y * 4 + along) * 2 + core


def device_of(column, zl):
    y = column // 8
    along = (column // 2) % 4
    x = along + (y % 2) * (3 - 2 * along)
    return y * 16 + zl * 8 + x * 2 + column % 2


def part_of(value):
    return (lax.broadcasted_iota(jnp.int32, value.shape, value.ndim - 1) // 32) % 2


def swap_parts(value):
    axis = value.ndim - 1
    return jnp.where(part_of(value) == 0, pltpu.roll(value, 96, axis), pltpu.roll(value, 32, axis))


def halves(value):
    high = value.astype(BF16)
    low = (value - high.astype(F32)).astype(BF16)
    return high, low


def body(src, dif, out, *refs):
    (fwd, inv, back, recv, top, bottom, kap, knear, kwide, kfold, plink, qplus, qminus,
     gr, gs, gi, lhs, sr, si, pack_l, pack_r, got_l, got_r, send) = refs[:24]
    fr, fi = refs[24 : 24 + SWEEPS], refs[24 + SWEEPS : 24 + 2 * SWEEPS]
    (in_send, in_recv, z_send, z_recv, k_send, k_recv, c_send, c_recv, out_send, out_recv,
     near_sem, mine_sem, plane_sem) = refs[24 + 2 * SWEEPS :]
    t = lax.axis_index("tm")
    s = lax.axis_index("space")
    y, zl, x, core = place(t)
    col = column_of(t)
    z = s * 2 + zl

    def z_device(step):
        other = (z + step + 8) % 8
        return (t + (other % 2 - zl) * 8, other // 2)

    outer = z_device(2 * zl - 1)

    def tile(index):
        return pl.ds(pl.multiple_of(index * COLS, COLS), COLS)

    def rows16(index):
        return pl.ds(pl.multiple_of(index * ROWS, ROWS), ROWS)

    barrier = pltpu.get_barrier_semaphore()

    for dy, dz, dx, dc in GREETED:
        there = ((y + dy) % 4) * 16 + ((zl + dz) % 2) * 8 + ((x + dx) % 4) * 2 + (core + dc) % 2
        pl.semaphore_signal(barrier, inc=1, device_id=(there, s), device_id_type=MESH)

    above, below = z > 0, z < 7
    has_outer = above & below

    @pl.when(has_outer)
    def _():
        pl.semaphore_signal(barrier, inc=1, device_id=outer, device_id_type=MESH)

    loads = [
        pltpu.make_async_copy(
            dif.at[pl.ds(pl.multiple_of(zl * 8, 8), 24), tile((col + 31 + d) % 32)],
            knear.at[:, pl.ds(d * COLS, COLS)],
            near_sem.at[d],
        )
        for d in range(3)
    ]
    for c in loads:
        c.start()
    pl.semaphore_wait(barrier, STEPS // 2 + has_outer.astype(jnp.int32))
    pl.semaphore_signal(
        plane_sem, inc=1, device_id=(t + 8 - 16 * zl, s), device_id_type=MESH
    )

    def arriving(p):
        _, pzl, _, _ = place(p)
        return pltpu.make_async_remote_copy(
            src_ref=src.at[rows16(pzl), tile(column_of(p))],
            dst_ref=recv.at[t],
            send_sem=in_send, recv_sem=in_recv.at[t // 8],
            device_id=(p, s), device_id_type=MESH,
        )

    krow = pl.ds(pl.multiple_of(zl * 24, 8), 8)
    kcopies = [
        pltpu.make_async_remote_copy(
            src_ref=dif.at[krow, tile((col + 31 + d) % 32)],
            dst_ref=kap.at[:, pl.ds(d * COLS, COLS)],
            send_sem=k_send.at[d], recv_sem=k_recv.at[d],
            device_id=outer, device_id_type=MESH,
        )
        for d in range(3)
    ]
    @pl.when(has_outer)
    def _():
        for c in kcopies:
            c.start()


    def in_plane(d, plane):
        turned = (y * 8 + x * 2 + core + d) % 32
        return (turned // 8) * 16 + plane * 8 + turned % 8

    @pl.loop(1, STEPS // 2)
    def _(d):
        arriving(in_plane(d, zl)).start()

    pl.semaphore_wait(plane_sem, 1)

    @pl.loop(0, STEPS // 2)
    def _(d):
        arriving(in_plane(d, 1 - zl)).start()

    own = pltpu.make_async_copy(src.at[rows16(zl), tile(col)], recv.at[t], in_recv.at[t // 8])
    own.start()

    def blocks(count, send_sem, recv_sem):
        some = recv.at[pl.ds(0, count)]
        return pltpu.make_async_remote_copy(
            src_ref=some, dst_ref=some, send_sem=send_sem, recv_sem=recv_sem,
            device_id=outer, device_id_type=MESH,
        )

    def link(j):
        here = kfold[j, INNER, :]
        south = 0.5 * (here + kfold[j + 1, INNER, :])
        east = 0.5 * (here + kfold[j, pl.ds(PAD + 1, WIDE), :])
        west = 0.5 * (here + kfold[j, pl.ds(PAD - 1, WIDE), :])
        plink[j + 1] = south
        qplus[j] = east
        qminus[j] = west
        total = step_ratio * (plink[j] + south + east + west)
        inside = jnp.where(here > 0.0, damping * step_ratio, 0.0)
        diag = lam_re + total
        scale = inside / (diag * diag + lam_im * lam_im)
        gr[j] = scale * diag
        gi[j] = scale * lam_im
        diag = lam_other + total
        gs[j] = inside * diag / (diag * diag + lam_im * lam_im)

    def gather_coefficients():
        for c in loads:
            c.wait()
        @pl.when(has_outer)
        def _():
            for c in kcopies:
                c.wait()

        row_id = lax.broadcasted_iota(jnp.int32, (32, COLS), 0)
        low_ok = jnp.where(z > 0, 0, 8)
        high_ok = jnp.where(z < 7, 32, 24)
        for d in range(3):
            near24 = knear[:, d * COLS : (d + 1) * COLS]
            far8 = kap[:, d * COLS : (d + 1) * COLS]
            strip = jnp.where(
                zl == 0, jnp.concatenate([far8, near24], 0), jnp.concatenate([near24, far8], 0)
            )
            keep = (row_id >= low_ok) & (row_id < high_ok)
            if d == 0:
                keep = keep & (col > 0)
            if d == 2:
                keep = keep & (col < 31)
            strip = jnp.where(keep, strip, 0.0)
            strip = jnp.concatenate([strip, jnp.zeros((96, COLS), F32)], 0)
            kwide[pl.ds(d * COLS, COLS), :] = strip.T
        for at in (pl.ds(0, PAD), pl.ds(PAD + WIDE, PAD)):
            kfold[:, at, :] = jnp.zeros((FOLD + 1, PAD, 128), F32)
        lane = lax.broadcasted_iota(jnp.int32, (WIDE, 128), 1)
        is_a = lane < 64
        is_0 = lane % 64 < 32
        part0 = kwide[pl.ds(COLS - 8, WIDE), :]
        part1 = kwide[pl.ds(COLS + 56, WIDE), :]
        for j in range(FOLD):
            k = 31 - j
            kfold[j, INNER, :] = jnp.where(
                is_a,
                jnp.where(is_0, part0[:, j : j + 1], part1[:, j : j + 1]),
                jnp.where(is_0, part0[:, k : k + 1], part1[:, k : k + 1]),
            )
        kfold[FOLD, INNER, :] = pltpu.roll(kfold[FOLD - 1, INNER, :], 64, 1)

    def clear_edges():
        for missing, ref in ((z == 0, top), (z == 7, bottom)):

            @pl.when(missing)
            def _():
                ref[...] = jnp.zeros(ref.shape, F32)

        edge = jnp.zeros((FOLD + 1, PAD, 128), F32)
        for ref in fr[:-1] + fi[:-1]:
            ref[:, pl.ds(0, PAD), :] = edge
            ref[:, pl.ds(PAD + WIDE, PAD), :] = edge

    slot = iota((1, 128), 1) % HALF
    root = circulant_alpha ** (1.0 / STEPS)
    theta = slot.astype(F32) * (2.0 * math.pi / STEPS)
    lam_re = 1.0 - root * jnp.cos(theta)
    lam_im = root * jnp.sin(theta)
    lam_other = jnp.where(slot == 0, 1.0 + root, lam_re)


    def links(first, last):
        @pl.loop(first, last)
        def _(j):
            link(j)

    def prepare(phase):
        if phase == 0:
            gather_coefficients()
            plink[0] = kfold[0, INNER, :]
        elif phase < 5:
            links(4 * phase - 4, 4 * phase)
        elif phase == 5:
            clear_edges()
        elif phase == 6:
            fill_forward(fwd)

    zcopies = []
    for phase in range(8):
        prepare(phase)
        group = ((y + 3 - phase % 4) % 4) * 2 + (zl + phase // 4) % 2
        blocks(8, in_send, in_recv.at[group]).wait_recv()
        steps = pl.ds(group * 8, 8)
        pair = [
            pltpu.make_async_remote_copy(
                src_ref=recv.at[steps, pl.ds(0, 8), :], dst_ref=bottom.at[steps],
                send_sem=z_send.at[phase, 0], recv_sem=z_recv.at[phase, 0],
                device_id=z_device(-1), device_id_type=MESH,
            ),
            pltpu.make_async_remote_copy(
                src_ref=recv.at[steps, pl.ds(8, 8), :], dst_ref=top.at[steps],
                send_sem=z_send.at[phase, 1], recv_sem=z_recv.at[phase, 1],
                device_id=z_device(1), device_id_type=MESH,
            ),
        ]
        zcopies.append(pair)
        pl.when(above)(pair[0].start)
        pl.when(below)(pair[1].start)

    left = device_of((col + 31) % 32, zl)
    right = device_of((col + 1) % 32, zl)

    def fold_in(i, first, second):
        high, low = halves(jnp.concatenate([first, second], 0).T)
        pieces = [high[:64], high[64:], low[:64], low[64:], high[:64], high[64:]]
        lhs[pl.ds(i * 64, 64), :] = jnp.concatenate(pieces, 1)

    def transformed(start, stage):
        for k in range(0, 8, PIECE):
            rows = lhs[pl.ds(64 * k, 64 * PIECE), :]
            result = jnp.dot(rows, fwd[...], preferred_element_type=F32)
            some = pl.ds(start + k, PIECE)
            sr[some, pl.ds(8, 64), :] = result[:, :128].reshape(PIECE, 64, 128)
            si[some, pl.ds(8, 64), :] = result[:, 128:].reshape(PIECE, 64, 128)
        mine = pl.ds(start, 8)
        re, im = sr[mine, pl.ds(8, 8), :], si[mine, pl.ds(8, 8), :]
        pack_l[mine] = jnp.where(part_of(re) == 0, re, swap_parts(im))
        re, im = sr[mine, pl.ds(64, 8), :], si[mine, pl.ds(64, 8), :]
        pack_r[mine] = jnp.where(part_of(re) == 1, re, swap_parts(im))
        copies = [
            pltpu.make_async_remote_copy(
                src_ref=pack_l.at[mine], dst_ref=got_r.at[mine],
                send_sem=c_send.at[stage, 0], recv_sem=c_recv.at[stage, 0],
                device_id=(left, s), device_id_type=MESH,
            ),
            pltpu.make_async_remote_copy(
                src_ref=pack_r.at[mine], dst_ref=got_l.at[mine],
                send_sem=c_send.at[stage, 1], recv_sem=c_recv.at[stage, 1],
                device_id=(right, s), device_id_type=MESH,
            ),
        ]
        for c in copies:
            c.start()
        return copies

    def join(j, from_left, from_right):
        re, im = sr[j, pl.ds(64, 8), :], si[j, pl.ds(64, 8), :]
        part = part_of(re)
        sr[j, pl.ds(0, 8), :] = swap_parts(jnp.where(part == 1, from_left, re))
        si[j, pl.ds(0, 8), :] = jnp.where(part == 0, from_left, swap_parts(im))
        re, im = sr[j, pl.ds(8, 8), :], si[j, pl.ds(8, 8), :]
        sr[j, pl.ds(72, 8), :] = swap_parts(jnp.where(part == 0, from_right, re))
        si[j, pl.ds(72, 8), :] = jnp.where(part == 1, from_right, swap_parts(im))

    def first_level(j, start, size):
        at = pl.ds(start, size)
        re, im, cross = sr[j, at, :], si[j, at, :], gi[j, at, :]
        fr[0][j, pl.ds(PAD + start, size), :] = gr[j, at, :] * re + cross * im
        fi[0][j, pl.ds(PAD + start, size), :] = gs[j, at, :] * im - cross * re

    def seam(level):
        for ref in (fr[level], fi[level]):
            ref[FOLD, INNER, :] = pltpu.roll(ref[FOLD - 1, INNER, :], 64, 1)

    def sweep(level, first, last, edges=False):
        pr, pi, nr, ni = fr[level - 1], fi[level - 1], fr[level], fi[level]
        if level == SWEEPS - 1:
            spans = ((8, 8), (64, 8)) if edges else ((8, 32), (40, 32))
        else:
            spans = ((0, 16), (64, 16)) if edges else ((0, 40), (40, 40))

        @pl.loop(first, last, unroll=7 if edges else (last - first if first >= 9 else 7))
        def _(j):
            for start, size in spans:
                at, mid = pl.ds(start, size), pl.ds(PAD + start, size)
                west, east = pl.ds(PAD - 1 + start, size), pl.ds(PAD + 1 + start, size)
                p0, p1, q0, q1 = plink[j, at, :], plink[j + 1, at, :], qminus[j, at, :], qplus[j, at, :]
                vr = sr[j, at, :] + p0 * pr[j - 1, mid, :] + p1 * pr[j + 1, mid, :]
                vr = vr + (q0 * pr[j, west, :] + q1 * pr[j, east, :])
                vi = si[j, at, :] + p0 * pi[j - 1, mid, :] + p1 * pi[j + 1, mid, :]
                vi = vi + (q0 * pi[j, west, :] + q1 * pi[j, east, :])
                cross = gi[j, at, :]
                nr[j, mid, :] = (1.0 - damping) * pr[j, mid, :] + (gr[j, at, :] * vr + cross * vi)
                ni[j, mid, :] = (1.0 - damping) * pi[j, mid, :] + (gs[j, at, :] * vi - cross * vr)

    recv2 = recv.reshape(STEPS * ROWS, COLS)

    for i in range(8):
        fold_in(i, recv2[pl.ds(i, STEPS, stride=ROWS), :], recv2[pl.ds(15 - i, STEPS, stride=ROWS), :])

    inside = transformed(8, 0)
    fill_inverse(inv)
    for c in inside:
        c.wait()

    @pl.loop(8, FOLD, unroll=8)
    def _(j):
        join(j, got_l[j], got_r[j])
        first_level(j, 0, WIDE)

    seam(0)
    for level in range(1, SWEEPS):
        sweep(level, 8 + level, FOLD)
        if level < SWEEPS - 1:
            seam(level)

    for up, down in zcopies:

        @pl.when(above)
        def _():
            up.wait_send()
            down.wait_recv()

        @pl.when(below)
        def _():
            down.wait_send()
            up.wait_recv()

    top2 = top.reshape(STEPS * 8, COLS)
    bottom2 = bottom.reshape(STEPS * 8, COLS)

    for h in range(8):
        fold_in(h, top2[pl.ds(h, STEPS, stride=8), :], bottom2[pl.ds(7 - h, STEPS, stride=8), :])

    outside = transformed(0, 1)

    @pl.loop(0, 8, unroll=8)
    def _(j):
        nothing = jnp.zeros((8, 128), F32)
        join(j, nothing, nothing)
        first_level(j, 0, WIDE)

    for level in range(1, SWEEPS):
        sweep(level, level + 1, 8 + level)
    for c in outside:
        c.wait()

    @pl.loop(0, 8, unroll=8)
    def _(j):
        join(j, got_l[j], got_r[j])
        first_level(j, 0, 16)
        first_level(j, 64, 16)

    for level in range(1, SWEEPS):
        sweep(level, level + 1, 8 + level, edges=True)

    send2 = send.reshape(STEPS * ROWS, COLS)
    middle = pl.ds(PAD + 8, 64)

    def rows64(i):
        return pl.ds(i * 64, 64)

    for i in range(8):
        high, low = halves(jnp.concatenate([fr[-1][8 + i, middle, :], fi[-1][8 + i, middle, :]], 1))
        lhs[rows64(i), :] = jnp.concatenate([high, low, high], 1)

    for k in range(0, 8, PIECE):
        some = pl.ds(64 * k, 64 * PIECE)
        back[some, :] = jnp.dot(lhs[some, :], inv[...], preferred_element_type=F32)

    for i in range(8):
        both = back[rows64(i), :]
        both = jnp.concatenate([both[:, :128], both[:, 128:]], 0).T
        send2[pl.ds(i, STEPS, stride=ROWS), :] = both[:STEPS]
        send2[pl.ds(15 - i, STEPS, stride=ROWS), :] = both[STEPS:]

    def leaving(p):
        return pltpu.make_async_remote_copy(
            src_ref=send.at[p],
            dst_ref=out.at[rows16(zl), tile(col)],
            send_sem=out_send, recv_sem=out_recv,
            device_id=(p, s), device_id_type=MESH,
        )

    @pl.loop(1, STEPS)
    def _(d):
        leaving((t + d) % STEPS).start()

    mine = pltpu.make_async_copy(send.at[t], out.at[rows16(zl), tile(col)], mine_sem)
    mine.start()
    blocks(STEPS - 1, in_send, out_recv).wait_send()
    blocks(STEPS - 1, out_send, out_recv).wait_send()
    blocks(STEPS - 1, out_send, out_recv).wait_recv()
    mine.wait()


def per_device(source, diffusivity):
    dma = pltpu.SemaphoreType.DMA

    def vmem(*shape):
        return pltpu.VMEM(shape, F32)

    level = vmem(FOLD + 1, WIDE + 2 * PAD, 128)
    plane = vmem(FOLD, WIDE, 128)
    edge = vmem(FOLD, 8, 128)
    result = pl.pallas_call(
        body,
        out_shape=jax.ShapeDtypeStruct(source.shape[1:], F32),
        in_specs=[pl.BlockSpec(memory_space=pl.ANY)] * 2,
        out_specs=pl.BlockSpec(memory_space=pl.ANY),
        scratch_shapes=[
            pltpu.VMEM((768, 256), BF16), pltpu.VMEM((768, 256), BF16), vmem(512, 256),
            vmem(STEPS, ROWS, COLS), vmem(STEPS, 8, COLS), vmem(STEPS, 8, COLS),
            vmem(8, 3 * COLS), vmem(24, 3 * COLS), vmem(3 * COLS, 128),
            level, vmem(FOLD + 1, WIDE, 128), plane, plane, plane, plane, plane,
            pltpu.VMEM((512, 768), BF16), plane, plane, edge, edge, edge, edge,
            vmem(STEPS, ROWS, COLS),
        ]
        + [level] * (2 * SWEEPS)
        + [
            dma, dma((8,)), dma((8, 2)), dma((8, 2)), dma((3,)), dma((3,)), dma((2, 2)), dma((2, 2)),
            dma, dma, dma((3,)), dma, pltpu.SemaphoreType.REGULAR,
        ],
        compiler_params=pltpu.CompilerParams(
            collective_id=0, has_side_effects=True, vmem_limit_bytes=425 * 2**17
        ),
        cost_estimate=pl.CostEstimate(flops=10**8, bytes_accessed=2**21, transcendentals=0),
    )(source[0], diffusivity)
    return result[None]


def solution(mesh):
    return jax.shard_map(
        per_device,
        mesh=mesh,
        in_specs=(P("tm", "space", None), P("space", None)),
        out_specs=P("tm", "space", None),
        check_vma=False,
    )
```

```python
import math

import jax
import jax.numpy as jnp
from jax import lax
from jax.experimental import pallas as pl
from jax.experimental.pallas import tpu as pltpu
from jax.sharding import PartitionSpec as P

SWEEPS = 8
STEPS = 64
circulant_alpha = 0.01
step_ratio = 4.0
damping = 0.8

MESH = pl.DeviceIdType.MESH
F32 = jnp.float32
BF16 = jnp.bfloat16
ROWS = 16
COLS = 128
HALF = STEPS // 2
FOLD = 16
WIDE = 80
PAD = 8
PIECE = 2
INNER = pl.ds(PAD, WIDE)


def iota(shape, axis):
    return lax.broadcasted_iota(jnp.int32, shape, axis)


def wave(steps, freq, imaginary):
    turn = jnp.where(imaginary, jnp.where(freq == 0, HALF * steps, steps * freq + STEPS // 4), steps * freq)
    return jnp.cos((turn % STEPS).astype(F32) * (2.0 * math.pi / STEPS))


def power(steps, sign):
    return jnp.exp(steps.astype(F32) * (sign * math.log(circulant_alpha) / STEPS))


def fill_forward(ref):
    shape = (STEPS, 8 * HALF)
    lane = iota(shape, 1)
    steps = iota(shape, 0)
    table = wave(steps, lane % HALF, lane >= 4 * HALF) * power(steps, 1.0) * (1.0 / step_ratio)
    for block in range(4):
        mine = (lane // HALF) % 4 == (block % 2) * 2 + block // 2
        high, low = halves(jnp.where(mine, table, 0.0))
        for base, value in ((0, high), (256, high), (512, low)):
            ref[pl.ds(base + block * STEPS, STEPS), :] = value


def fill_inverse(ref):
    shape = (4 * HALF, 4 * STEPS)
    row = iota(shape, 0)
    lane = iota(shape, 1)
    freq, steps, block = row % HALF, lane % STEPS, lane // STEPS
    mine = row // HALF == (block % 2) * 2 + block // 2
    scale = power(steps, -1.0) * jnp.where(mine, jnp.where(freq == 0, 1.0, 2.0) / STEPS, 0.0)
    for plane in range(2):
        high, low = halves(wave(steps, freq, plane == 1) * scale)
        for base, value in ((0, high), (256, high), (512, low)):
            ref[pl.ds(base + plane * 128, 128), :] = value


def offsets():
    every = [(y, z, x, c) for y in range(4) for z in range(2) for x in range(4) for c in range(2)]
    return sorted(every[1:], key=lambda o: -(min(o[0], 4 - o[0]) + o[1] + min(o[2], 4 - o[2])))


FARTHEST = offsets()
GREETED = [o for o in FARTHEST if o[1] == 0 or sum(o) == 1]


def place(t):
    return t // 16, (t // 8) % 2, (t // 2) % 4, t % 2


def column_of(t):
    y, _, x, core = place(t)
    along = x + (y % 2) * (3 - 2 * x)
    return (y * 4 + along) * 2 + core


def device_of(column, zl):
    y = column // 8
    along = (column // 2) % 4
    x = along + (y % 2) * (3 - 2 * along)
    return y * 16 + zl * 8 + x * 2 + column % 2


def part_of(value):
    return (lax.broadcasted_iota(jnp.int32, value.shape, value.ndim - 1) // 32) % 2


def swap_parts(value):
    axis = value.ndim - 1
    return jnp.where(part_of(value) == 0, pltpu.roll(value, 96, axis), pltpu.roll(value, 32, axis))


def halves(value):
    high = value.astype(BF16)
    low = (value - high.astype(F32)).astype(BF16)
    return high, low


def body(src, dif, out, *refs):
    (fwd, inv, back, recv, top, bottom, kap, knear, kwide, kfold, plink, qplus, qminus,
     gr, gs, gi, lhs, sr, si, pack_l, pack_r, got_l, got_r, send) = refs[:24]
    fr, fi = refs[24 : 24 + SWEEPS], refs[24 + SWEEPS : 24 + 2 * SWEEPS]
    (in_send, in_recv, z_send, z_recv, k_send, k_recv, c_send, c_recv, out_send, out_recv,
     near_sem, mine_sem, plane_sem) = refs[24 + 2 * SWEEPS :]
    t = lax.axis_index("tm")
    s = lax.axis_index("space")
    y, zl, x, core = place(t)
    col = column_of(t)
    z = s * 2 + zl

    def z_device(step):
        other = (z + step + 8) % 8
        return (t + (other % 2 - zl) * 8, other // 2)

    outer = z_device(2 * zl - 1)

    def tile(index):
        return pl.ds(pl.multiple_of(index * COLS, COLS), COLS)

    def rows16(index):
        return pl.ds(pl.multiple_of(index * ROWS, ROWS), ROWS)

    barrier = pltpu.get_barrier_semaphore()

    for dy, dz, dx, dc in GREETED:
        there = ((y + dy) % 4) * 16 + ((zl + dz) % 2) * 8 + ((x + dx) % 4) * 2 + (core + dc) % 2
        pl.semaphore_signal(barrier, inc=1, device_id=(there, s), device_id_type=MESH)

    above, below = z > 0, z < 7
    has_outer = above & below

    @pl.when(has_outer)
    def _():
        pl.semaphore_signal(barrier, inc=1, device_id=outer, device_id_type=MESH)

    loads = [
        pltpu.make_async_copy(
            dif.at[pl.ds(pl.multiple_of(zl * 8, 8), 24), tile((col + 31 + d) % 32)],
            knear.at[:, pl.ds(d * COLS, COLS)],
            near_sem.at[d],
        )
        for d in range(3)
    ]
    for c in loads:
        c.start()
    pl.semaphore_wait(barrier, STEPS // 2 + has_outer.astype(jnp.int32))
    pl.semaphore_signal(
        plane_sem, inc=1, device_id=(t + 8 - 16 * zl, s), device_id_type=MESH
    )

    def arriving(p):
        _, pzl, _, _ = place(p)
        return pltpu.make_async_remote_copy(
            src_ref=src.at[rows16(pzl), tile(column_of(p))],
            dst_ref=recv.at[t],
            send_sem=in_send, recv_sem=in_recv.at[t // 8],
            device_id=(p, s), device_id_type=MESH,
        )

    krow = pl.ds(pl.multiple_of(zl * 24, 8), 8)
    kcopies = [
        pltpu.make_async_remote_copy(
            src_ref=dif.at[krow, tile((col + 31 + d) % 32)],
            dst_ref=kap.at[:, pl.ds(d * COLS, COLS)],
            send_sem=k_send.at[d], recv_sem=k_recv.at[d],
            device_id=outer, device_id_type=MESH,
        )
        for d in range(3)
    ]
    @pl.when(has_outer)
    def _():
        for c in kcopies:
            c.start()


    def in_plane(d, plane):
        turned = (y * 8 + x * 2 + core + d) % 32
        return (turned // 8) * 16 + plane * 8 + turned % 8

    @pl.loop(1, STEPS // 2)
    def _(d):
        arriving(in_plane(d, zl)).start()

    pl.semaphore_wait(plane_sem, 1)

    @pl.loop(0, STEPS // 2)
    def _(d):
        arriving(in_plane(d, 1 - zl)).start()

    own = pltpu.make_async_copy(src.at[rows16(zl), tile(col)], recv.at[t], in_recv.at[t // 8])
    own.start()

    def blocks(count, send_sem, recv_sem):
        some = recv.at[pl.ds(0, count)]
        return pltpu.make_async_remote_copy(
            src_ref=some, dst_ref=some, send_sem=send_sem, recv_sem=recv_sem,
            device_id=outer, device_id_type=MESH,
        )

    def link(j):
        here = kfold[j, INNER, :]
        south = 0.5 * (here + kfold[j + 1, INNER, :])
        east = 0.5 * (here + kfold[j, pl.ds(PAD + 1, WIDE), :])
        west = 0.5 * (here + kfold[j, pl.ds(PAD - 1, WIDE), :])
        plink[j + 1] = south
        qplus[j] = east
        qminus[j] = west
        total = step_ratio * (plink[j] + south + east + west)
        inside = jnp.where(here > 0.0, damping * step_ratio, 0.0)
        diag = lam_re + total
        scale = inside / (diag * diag + lam_im * lam_im)
        gr[j] = scale * diag
        gi[j] = scale * lam_im
        diag = lam_other + total
        gs[j] = inside * diag / (diag * diag + lam_im * lam_im)

    def gather_coefficients():
        for c in loads:
            c.wait()
        @pl.when(has_outer)
        def _():
            for c in kcopies:
                c.wait()

        row_id = lax.broadcasted_iota(jnp.int32, (32, COLS), 0)
        low_ok = jnp.where(z > 0, 0, 8)
        high_ok = jnp.where(z < 7, 32, 24)
        for d in range(3):
            near24 = knear[:, d * COLS : (d + 1) * COLS]
            far8 = kap[:, d * COLS : (d + 1) * COLS]
            strip = jnp.where(
                zl == 0, jnp.concatenate([far8, near24], 0), jnp.concatenate([near24, far8], 0)
            )
            keep = (row_id >= low_ok) & (row_id < high_ok)
            if d == 0:
                keep = keep & (col > 0)
            if d == 2:
                keep = keep & (col < 31)
            strip = jnp.where(keep, strip, 0.0)
            strip = jnp.concatenate([strip, jnp.zeros((96, COLS), F32)], 0)
            kwide[pl.ds(d * COLS, COLS), :] = strip.T
        for at in (pl.ds(0, PAD), pl.ds(PAD + WIDE, PAD)):
            kfold[:, at, :] = jnp.zeros((FOLD + 1, PAD, 128), F32)
        lane = lax.broadcasted_iota(jnp.int32, (WIDE, 128), 1)
        is_a = lane < 64
        is_0 = lane % 64 < 32
        part0 = kwide[pl.ds(COLS - 8, WIDE), :]
        part1 = kwide[pl.ds(COLS + 56, WIDE), :]
        for j in range(FOLD):
            k = 31 - j
            kfold[j, INNER, :] = jnp.where(
                is_a,
                jnp.where(is_0, part0[:, j : j + 1], part1[:, j : j + 1]),
                jnp.where(is_0, part0[:, k : k + 1], part1[:, k : k + 1]),
            )
        kfold[FOLD, INNER, :] = pltpu.roll(kfold[FOLD - 1, INNER, :], 64, 1)

    def clear_edges():
        for missing, ref in ((z == 0, top), (z == 7, bottom)):

            @pl.when(missing)
            def _():
                ref[...] = jnp.zeros(ref.shape, F32)

        edge = jnp.zeros((FOLD + 1, PAD, 128), F32)
        for ref in fr[:-1] + fi[:-1]:
            ref[:, pl.ds(0, PAD), :] = edge
            ref[:, pl.ds(PAD + WIDE, PAD), :] = edge

    slot = iota((1, 128), 1) % HALF
    root = circulant_alpha ** (1.0 / STEPS)
    theta = slot.astype(F32) * (2.0 * math.pi / STEPS)
    lam_re = 1.0 - root * jnp.cos(theta)
    lam_im = root * jnp.sin(theta)
    lam_other = jnp.where(slot == 0, 1.0 + root, lam_re)


    def links(first, last):
        @pl.loop(first, last)
        def _(j):
            link(j)

    def prepare(phase):
        if phase == 0:
            gather_coefficients()
            plink[0] = kfold[0, INNER, :]
        elif phase < 5:
            links(4 * phase - 4, 4 * phase)
        elif phase == 5:
            clear_edges()
        elif phase == 6:
            fill_forward(fwd)

    zcopies = []
    for phase in range(8):
        prepare(phase)
        group = ((y + 3 - phase % 4) % 4) * 2 + (zl + phase // 4) % 2
        blocks(8, in_send, in_recv.at[group]).wait_recv()
        steps = pl.ds(group * 8, 8)
        pair = [
            pltpu.make_async_remote_copy(
                src_ref=recv.at[steps, pl.ds(0, 8), :], dst_ref=bottom.at[steps],
                send_sem=z_send.at[phase, 0], recv_sem=z_recv.at[phase, 0],
                device_id=z_device(-1), device_id_type=MESH,
            ),
            pltpu.make_async_remote_copy(
                src_ref=recv.at[steps, pl.ds(8, 8), :], dst_ref=top.at[steps],
                send_sem=z_send.at[phase, 1], recv_sem=z_recv.at[phase, 1],
                device_id=z_device(1), device_id_type=MESH,
            ),
        ]
        zcopies.append(pair)
        pl.when(above)(pair[0].start)
        pl.when(below)(pair[1].start)

    left = device_of((col + 31) % 32, zl)
    right = device_of((col + 1) % 32, zl)

    def fold_in(i, first, second):
        high, low = halves(jnp.concatenate([first, second], 0).T)
        pieces = [high[:64], high[64:], low[:64], low[64:], high[:64], high[64:]]
        lhs[pl.ds(i * 64, 64), :] = jnp.concatenate(pieces, 1)

    def transformed(start, stage):
        for k in range(0, 8, PIECE):
            rows = lhs[pl.ds(64 * k, 64 * PIECE), :]
            result = jnp.dot(rows, fwd[...], preferred_element_type=F32)
            some = pl.ds(start + k, PIECE)
            sr[some, pl.ds(8, 64), :] = result[:, :128].reshape(PIECE, 64, 128)
            si[some, pl.ds(8, 64), :] = result[:, 128:].reshape(PIECE, 64, 128)
        mine = pl.ds(start, 8)
        re, im = sr[mine, pl.ds(8, 8), :], si[mine, pl.ds(8, 8), :]
        pack_l[mine] = jnp.where(part_of(re) == 0, re, swap_parts(im))
        re, im = sr[mine, pl.ds(64, 8), :], si[mine, pl.ds(64, 8), :]
        pack_r[mine] = jnp.where(part_of(re) == 1, re, swap_parts(im))
        copies = [
            pltpu.make_async_remote_copy(
                src_ref=pack_l.at[mine], dst_ref=got_r.at[mine],
                send_sem=c_send.at[stage, 0], recv_sem=c_recv.at[stage, 0],
                device_id=(left, s), device_id_type=MESH,
            ),
            pltpu.make_async_remote_copy(
                src_ref=pack_r.at[mine], dst_ref=got_l.at[mine],
                send_sem=c_send.at[stage, 1], recv_sem=c_recv.at[stage, 1],
                device_id=(right, s), device_id_type=MESH,
            ),
        ]
        for c in copies:
            c.start()
        return copies

    def join(j, from_left, from_right):
        re, im = sr[j, pl.ds(64, 8), :], si[j, pl.ds(64, 8), :]
        part = part_of(re)
        sr[j, pl.ds(0, 8), :] = swap_parts(jnp.where(part == 1, from_left, re))
        si[j, pl.ds(0, 8), :] = jnp.where(part == 0, from_left, swap_parts(im))
        re, im = sr[j, pl.ds(8, 8), :], si[j, pl.ds(8, 8), :]
        sr[j, pl.ds(72, 8), :] = swap_parts(jnp.where(part == 0, from_right, re))
        si[j, pl.ds(72, 8), :] = jnp.where(part == 1, from_right, swap_parts(im))

    def first_level(j, start, size):
        at = pl.ds(start, size)
        re, im, cross = sr[j, at, :], si[j, at, :], gi[j, at, :]
        fr[0][j, pl.ds(PAD + start, size), :] = gr[j, at, :] * re + cross * im
        fi[0][j, pl.ds(PAD + start, size), :] = gs[j, at, :] * im - cross * re

    def seam(level):
        for ref in (fr[level], fi[level]):
            ref[FOLD, INNER, :] = pltpu.roll(ref[FOLD - 1, INNER, :], 64, 1)

    def sweep(level, first, last, edges=False):
        pr, pi, nr, ni = fr[level - 1], fi[level - 1], fr[level], fi[level]
        if level == SWEEPS - 1:
            spans = ((8, 8), (64, 8)) if edges else ((8, 32), (40, 32))
        else:
            spans = ((0, 16), (64, 16)) if edges else ((0, 40), (40, 40))

        @pl.loop(first, last, unroll=7 if edges else (last - first if first >= 9 else 7))
        def _(j):
            for start, size in spans:
                at, mid = pl.ds(start, size), pl.ds(PAD + start, size)
                west, east = pl.ds(PAD - 1 + start, size), pl.ds(PAD + 1 + start, size)
                p0, p1, q0, q1 = plink[j, at, :], plink[j + 1, at, :], qminus[j, at, :], qplus[j, at, :]
                vr = sr[j, at, :] + p0 * pr[j - 1, mid, :] + p1 * pr[j + 1, mid, :]
                vr = vr + (q0 * pr[j, west, :] + q1 * pr[j, east, :])
                vi = si[j, at, :] + p0 * pi[j - 1, mid, :] + p1 * pi[j + 1, mid, :]
                vi = vi + (q0 * pi[j, west, :] + q1 * pi[j, east, :])
                cross = gi[j, at, :]
                nr[j, mid, :] = (1.0 - damping) * pr[j, mid, :] + (gr[j, at, :] * vr + cross * vi)
                ni[j, mid, :] = (1.0 - damping) * pi[j, mid, :] + (gs[j, at, :] * vi - cross * vr)

    recv2 = recv.reshape(STEPS * ROWS, COLS)

    for i in range(8):
        fold_in(i, recv2[pl.ds(i, STEPS, stride=ROWS), :], recv2[pl.ds(15 - i, STEPS, stride=ROWS), :])

    inside = transformed(8, 0)
    fill_inverse(inv)
    for c in inside:
        c.wait()

    @pl.loop(8, FOLD, unroll=8)
    def _(j):
        join(j, got_l[j], got_r[j])
        first_level(j, 0, WIDE)

    seam(0)
    for level in range(1, SWEEPS):
        sweep(level, 8 + level, FOLD)
        if level < SWEEPS - 1:
            seam(level)

    for up, down in zcopies:

        @pl.when(above)
        def _():
            up.wait_send()
            down.wait_recv()

        @pl.when(below)
        def _():
            down.wait_send()
            up.wait_recv()

    top2 = top.reshape(STEPS * 8, COLS)
    bottom2 = bottom.reshape(STEPS * 8, COLS)

    for h in range(8):
        fold_in(h, top2[pl.ds(h, STEPS, stride=8), :], bottom2[pl.ds(7 - h, STEPS, stride=8), :])

    outside = transformed(0, 1)

    @pl.loop(0, 8, unroll=8)
    def _(j):
        nothing = jnp.zeros((8, 128), F32)
        join(j, nothing, nothing)
        first_level(j, 0, WIDE)

    for level in range(1, SWEEPS):
        sweep(level, level + 1, 8 + level)
    for c in outside:
        c.wait()

    @pl.loop(0, 8, unroll=8)
    def _(j):
        join(j, got_l[j], got_r[j])
        first_level(j, 0, 16)
        first_level(j, 64, 16)

    for level in range(1, SWEEPS):
        sweep(level, level + 1, 8 + level, edges=True)

    send2 = send.reshape(STEPS * ROWS, COLS)
    middle = pl.ds(PAD + 8, 64)

    def rows64(i):
        return pl.ds(i * 64, 64)

    for i in range(8):
        high, low = halves(jnp.concatenate([fr[-1][8 + i, middle, :], fi[-1][8 + i, middle, :]], 1))
        lhs[rows64(i), :] = jnp.concatenate([high, low, high], 1)

    for k in range(0, 8, PIECE):
        some = pl.ds(64 * k, 64 * PIECE)
        back[some, :] = jnp.dot(lhs[some, :], inv[...], preferred_element_type=F32)

    for i in range(8):
        both = back[rows64(i), :]
        both = jnp.concatenate([both[:, :128], both[:, 128:]], 0).T
        send2[pl.ds(i, STEPS, stride=ROWS), :] = both[:STEPS]
        send2[pl.ds(15 - i, STEPS, stride=ROWS), :] = both[STEPS:]

    def leaving(p):
        return pltpu.make_async_remote_copy(
            src_ref=send.at[p],
            dst_ref=out.at[rows16(zl), tile(col)],
            send_sem=out_send, recv_sem=out_recv,
            device_id=(p, s), device_id_type=MESH,
        )

    @pl.loop(1, STEPS)
    def _(d):
        leaving((t + d) % STEPS).start()

    mine = pltpu.make_async_copy(send.at[t], out.at[rows16(zl), tile(col)], mine_sem)
    mine.start()
    blocks(STEPS - 1, in_send, out_recv).wait_send()
    blocks(STEPS - 1, out_send, out_recv).wait_send()
    blocks(STEPS - 1, out_send, out_recv).wait_recv()
    mine.wait()


def per_device(source, diffusivity):
    dma = pltpu.SemaphoreType.DMA

    def vmem(*shape):
        return pltpu.VMEM(shape, F32)

    level = vmem(FOLD + 1, WIDE + 2 * PAD, 128)
    plane = vmem(FOLD, WIDE, 128)
    edge = vmem(FOLD, 8, 128)
    result = pl.pallas_call(
        body,
        out_shape=jax.ShapeDtypeStruct(source.shape[1:], F32),
        in_specs=[pl.BlockSpec(memory_space=pl.ANY)] * 2,
        out_specs=pl.BlockSpec(memory_space=pl.ANY),
        scratch_shapes=[
            pltpu.VMEM((768, 256), BF16), pltpu.VMEM((768, 256), BF16), vmem(512, 256),
            vmem(STEPS, ROWS, COLS), vmem(STEPS, 8, COLS), vmem(STEPS, 8, COLS),
            vmem(8, 3 * COLS), vmem(24, 3 * COLS), vmem(3 * COLS, 128),
            level, vmem(FOLD + 1, WIDE, 128), plane, plane, plane, plane, plane,
            pltpu.VMEM((512, 768), BF16), plane, plane, edge, edge, edge, edge,
            vmem(STEPS, ROWS, COLS),
        ]
        + [level] * (2 * SWEEPS)
        + [
            dma, dma((8,)), dma((8, 2)), dma((8, 2)), dma((3,)), dma((3,)), dma((2, 2)), dma((2, 2)),
            dma, dma, dma((3,)), dma, pltpu.SemaphoreType.REGULAR,
        ],
        compiler_params=pltpu.CompilerParams(
            collective_id=0, has_side_effects=True, vmem_limit_bytes=425 * 2**17
        ),
        cost_estimate=pl.CostEstimate(flops=10**8, bytes_accessed=2**21, transcendentals=0),
    )(source[0], diffusivity)
    return result[None]


def solution(mesh):
    return jax.shard_map(
        per_device,
        mesh=mesh,
        in_specs=(P("tm", "space", None), P("space", None)),
        out_specs=P("tm", "space", None),
        check_vma=False,
    )
```
